512 devices in a mesh: leaf: 16 (over z, core), clusters: 32 (over x, y).
Axes of the slice: x: 4, y: 8, z: 8, core: 2. Of those that a mesh axis runs over, the one named last changes fastest.
Arguments:
- samples: float32 [262144, 256], P(('clusters', 'leaf')), may hold values from -6 to 6
- probes: float32 [262144, 256], P(('clusters', 'leaf')), may hold values from -6 to 6
- near_blocks: float32 [262144, 2, 512], P(('clusters', 'leaf')), may hold values from -0.15625 to 0.15625
- couplings: float32 [32, 15, 2, 128, 128], P('clusters'), may hold values from -0.375 to 0.375
- node_slot: int32 [32, 15], P('clusters'), may hold values from 0 to 14, each once within a row
Outputs:
- leaf_bases: float32 [262144, 128], P(('clusters', 'leaf'))
- transfer_bases: float32 [512, 4, 256, 128], P(('clusters', 'leaf'))
- top_samples: float32 [32, 128, 256], P('clusters')
- top_probes: float32 [32, 128, 256], P('clusters')
The draws below stay inside these ranges and needn't reach their ends.
Inputs may be any that keep to these rules, and one draw needn't show every extreme that they name: Every row of node_slot names each of 0 to 14 exactly once.
All inputs are finite; a program needn't handle non-finite values.
Results may differ from the reference program's by a relative error of at most 0.00016.
Values sent between devices are 32-bit elements; how exact they have to be, the bound alone decides.
A program may use at most 64 MiB of HBM per device.

```python
import jax
import jax.numpy as jnp
from jax import lax

K = 128
S = 256
M = 512
SUBTREE = 16
LEVELS = 4
NODES = 15
ROWS = 262144
N_CLUSTERS = 32


def block_levels(own_key, shape, cuts, low, top_value):
    def one(axis_at, parts):
        draws = jax.random.uniform(jax.random.fold_in(jax.random.fold_in(own_key, 6), axis_at), (parts,), jnp.float32, low / len(cuts), top_value / len(cuts))
        return jnp.repeat(jnp.exp(draws), shape[axis_at] // parts).reshape((-1,) + (1,) * (len(shape) - axis_at - 1))

    factor_of = one(*cuts[0])
    for cut in cuts[1:]:
        factor_of = factor_of * one(*cut)
    return factor_of


def noise(rng, extent, width, reach, cuts=(), dtype=jnp.bfloat16):
    array = jax.random.normal(rng, extent, jnp.float32) * width
    if len(cuts) > 0:
        array = block_levels(rng, extent, cuts, -0.22, 0.18) * array
    return jnp.clip(array, min=-reach, max=reach).astype(dtype)


def setup_inputs(seed: int = 0) -> dict:
    keys = jax.random.split(jax.random.key(seed), 6)
    return {
        "samples": noise(keys[0], (ROWS, S), 1.0, 6.0, ((0, 512),), jnp.float32),
        "probes": noise(keys[1], (ROWS, S), 1.0, 6.0, ((0, 512),), jnp.float32),
        "near_blocks": noise(keys[2], (ROWS, 2, M), (3 * M) ** -0.5, 0.15625, ((0, 512),), jnp.float32),
        "couplings": noise(keys[3], (N_CLUSTERS, NODES, 2, K, K), (2 * K) ** -0.5, 0.375, ((0, 32),), jnp.float32),
        "node_slot": jax.vmap(lambda own: jax.random.permutation(own, NODES))(jax.random.split(keys[4], N_CLUSTERS)).reshape((N_CLUSTERS, NODES)).astype(jnp.int32),
    }


full_precision = lax.Precision.HIGHEST

def orthonormal(tall_block):
    gram_matrix = jnp.einsum('...rk,...rj->...kj', tall_block, tall_block, precision=full_precision)
    lower_factor = jnp.linalg.cholesky(gram_matrix)
    flipped = jax.scipy.linalg.solve_triangular(lower_factor, jnp.swapaxes(tall_block, -1, -2), lower=True)
    return jnp.swapaxes(flipped, -1, -2)

def project(node_basis, target):
    return jnp.einsum('...rk,...rs->...ks', node_basis, target, precision=full_precision)

def reference(samples, probes, near_blocks, couplings, node_slot):
    leaves = samples.shape[0] // M
    sample_blocks = samples.reshape(leaves, M, S)
    probe_blocks = probes.reshape(leaves, M, S)
    near_split = near_blocks.reshape(leaves, M, 2, M)
    zeros_block = jnp.zeros((1, M, S), jnp.float32)
    diag_term = jnp.einsum('tmn,tns->tms', near_split[:, :, 0, :], probe_blocks, precision=full_precision)
    next_blocks = jnp.concatenate([probe_blocks[1:], zeros_block], axis=0)
    upper_term = jnp.einsum('tmn,tns->tms', near_split[:, :, 1, :], next_blocks, precision=full_precision)
    lower_prod = jnp.einsum('tnm,tns->tms', near_split[:, :, 1, :], probe_blocks, precision=full_precision)
    lower_term = jnp.concatenate([zeros_block, lower_prod[:-1]], axis=0)
    far_samples = sample_blocks - diag_term - upper_term - lower_term
    leaf_basis = orthonormal(far_samples[:, :, :K])
    sample_coef = project(leaf_basis, far_samples)
    probe_coef = project(leaf_basis, probe_blocks)
    ancestors = []
    for level_index in range(1, LEVELS + 1):
        children = sample_coef.shape[0]
        parents = children // 2
        zeros_coef = jnp.zeros((2, K, S), jnp.float32)
        left_far = jnp.concatenate([zeros_coef, probe_coef[:-2]], axis=0)
        right_far = jnp.concatenate([probe_coef[2:], zeros_coef], axis=0)
        parity = (jnp.arange(children) % 2)[:, None, None]
        main_far = jnp.where(parity == 0, left_far, right_far)
        other_far = jnp.where(parity == 0, right_far, left_far)
        per_tree = SUBTREE >> level_index
        parent_ids = jnp.arange(parents)
        subtree_index = parent_ids // per_tree
        node_index = SUBTREE - (SUBTREE >> level_index - 1) + parent_ids % per_tree
        slot_index = node_slot[subtree_index, node_index]
        chosen = couplings[subtree_index, slot_index]
        child_coupling = chosen.reshape(children, K, K)
        main_term = jnp.einsum('tij,tjs->tis', child_coupling, main_far, precision=full_precision)
        other_term = jnp.einsum('tji,tjs->tis', child_coupling, other_far, precision=full_precision)
        corrected = sample_coef - main_term - other_term
        stacked = corrected.reshape(parents, 2 * K, S)
        stacked_probes = probe_coef.reshape(parents, 2 * K, S)
        node_basis = orthonormal(stacked[:, :, :K])
        ancestors.append(jnp.repeat(node_basis, 2 ** level_index, axis=0))
        sample_coef = project(node_basis, stacked)
        probe_coef = project(node_basis, stacked_probes)
    transfer_bases = jnp.stack(ancestors, axis=1)
    return (leaf_basis.reshape(leaves * M, K), transfer_bases, sample_coef, probe_coef)
```

```python
import functools

import jax
import jax.numpy as jnp
from jax import lax
from jax.experimental import pallas as pl
from jax.experimental.pallas import tpu as pltpu
from jax.sharding import PartitionSpec as P

MESH = pl.DeviceIdType.MESH
f32 = jnp.float32
bf16 = jnp.bfloat16

K = 128
ROWS = 512
BLOCK = 8
REACH = 3


def halves(value):
    high = value.astype(bf16)
    return high, (value - high.astype(f32)).astype(bf16)


def product(a, b, contract=(1, 0)):
    dims = (((contract[0],), (contract[1],)), ((), ()))
    a_high, a_low = halves(a)
    b_high, b_low = halves(b)
    dot = functools.partial(lax.dot_general, dimension_numbers=dims, preferred_element_type=f32)
    return dot(a_high, b_high) + (dot(a_high, b_low) + dot(a_low, b_high))


def spread(block, column):
    return jnp.broadcast_to(block[:, column : column + 1], (block.shape[0], K))


def inverse_factor(gram, interludes):
    panels = K // BLOCK
    lane = lax.broadcasted_iota(jnp.int32, (BLOCK, K), 1)
    sub = lax.broadcasted_iota(jnp.int32, (BLOCK, K), 0)
    rounded = lambda v: v.astype(bf16).astype(f32)
    rows = [gram[BLOCK * g : BLOCK * (g + 1)] for g in range(panels)]
    pivot = [spread(rows[0], i) for i in range(BLOCK)]
    done = []
    for k in range(panels):
        if k in interludes:
            interludes[k]()
        first, after = BLOCK * k, BLOCK * (k + 1)
        near_end = min(panels, k + 1 + REACH)
        inside = (lane >= first) & (lane < after)
        panel = jnp.where(inside, (lane == first + sub).astype(f32), rows[k])
        below = coming = upcoming = far = None
        if k + 1 < panels:
            below = [spread(rows[k + 1], first + i) for i in range(BLOCK)]
            coming = [spread(rows[k + 1], after + i) for i in range(BLOCK)]
            upcoming = jnp.where(inside, 0.0, rows[k + 1])
        if near_end > k + 2:
            block = jnp.concatenate(rows[k + 2 : near_end], axis=0)
            far = [spread(block, first + i) for i in range(BLOCK)]
            wide = lax.broadcasted_iota(jnp.int32, block.shape, 1)
            far_rows = jnp.where((wide >= first) & (wide < after), 0.0, block)
        for i in range(BLOCK):
            scale = lax.rsqrt(pivot[i][i : i + 1, :])
            column = pivot[i] * scale
            row = panel[i : i + 1, :] * scale
            entry = [column[j : j + 1, :] for j in range(BLOCK)]
            for j in range(i + 1, BLOCK):
                pivot[j] = pivot[j] - column * entry[j]
            panel = jnp.where(sub == i, row, panel - jnp.where(sub > i, column, 0.0) * row)
            if below is not None:
                lower = below[i] * scale
                for j in range(i + 1, BLOCK):
                    below[j] = below[j] - lower * entry[j]
                for j in range(BLOCK):
                    coming[j] = coming[j] - lower * lower[j : j + 1, :]
                upcoming = upcoming - lower * row
            if far is not None:
                lowest = far[i] * scale
                for j in range(i + 1, BLOCK):
                    far[j] = far[j] - lowest * entry[j]
                far_rows = far_rows - lowest * row
        done.append(jnp.where(lane < after, panel, 0.0))
        pivot = coming
        if below is not None:
            rows[k + 1] = upcoming
        if far is not None:
            for g in range(k + 2, near_end):
                rows[g] = far_rows[BLOCK * (g - k - 2) : BLOCK * (g - k - 1)]
        if near_end < panels:
            high = rounded(panel)
            middle = rounded(panel - high)
            low = rounded(panel - high - middle)
            left = jnp.concatenate([high, high, middle, high, low, middle], axis=0).astype(bf16)
            right = jnp.concatenate([high, middle, high, low, high, middle], axis=0).astype(bf16)
            update = lax.dot_general(
                left, right, (((0,), (0,)), ((), ())), preferred_element_type=f32
            )
            for g in range(near_end, panels):
                rows[g] = jnp.where(inside, 0.0, rows[g]) - update[BLOCK * g : BLOCK * (g + 1)]
    return jnp.concatenate(done, axis=0)


def when(condition, run):
    if isinstance(condition, bool):
        if condition:
            run()
    else:
        pl.when(condition)(run)


def kernel(
    leaves, subtrees, slots, samples, probes, near, couplings,
    leaf_out, transfer_out, top_samples, top_probes,
    near_v, probes_v, samples_v, couplings_v,
    next_probes, handed, handed_in, far1, gram, inverse,
    second, stack1, wside1, z2, stack2, wside2,
    w1_out, w2_out, e1_out, e2_out,
    w1_in, w2_in, sib_in, q_leaf, q_top,
    local_sem, leaf_send, leaf_recv, send_sem, recv_sem, out_sem,
):
    levels = leaves.bit_length() - 1
    total = leaves * subtrees
    member = lax.axis_index("leaf")
    mine = lax.axis_index("clusters") * leaves + member

    def peer(offset):
        index = lax.rem(mine + offset + total, total)
        return {"leaf": lax.rem(index, leaves), "clusters": index // leaves}

    def send(source, target, sems, offset):
        copy = pltpu.make_async_remote_copy(
            src_ref=source, dst_ref=target, send_sem=sems[0], recv_sem=sems[1],
            device_id=peer(offset), device_id_type=MESH,
        )
        return copy

    loads = [
        pltpu.make_async_copy(near, near_v, local_sem.at[0]),
        pltpu.make_async_copy(probes, probes_v, local_sem.at[1]),
        pltpu.make_async_copy(samples, samples_v, local_sem.at[2]),
        pltpu.make_async_copy(couplings, couplings_v, local_sem.at[3]),
    ]
    for load in loads:
        load.start()

    barrier = pltpu.get_barrier_semaphore()
    distances = [1 << i for i in range(levels + 1)]
    for distance in distances:
        for offset in (distance, -distance):
            pl.semaphore_signal(barrier, inc=1, device_id=peer(offset), device_id_type=MESH)
    pl.semaphore_wait(barrier, 2 * len(distances))

    def leaf_probes(half):
        return send(
            probes.at[:, K * half : K * (half + 1)], next_probes.at[half],
            (leaf_send.at[half], leaf_recv.at[half]), -1,
        )

    def leaf_handed(half):
        return send(
            handed.at[half], handed_in.at[half],
            (leaf_send.at[2 + half], leaf_recv.at[2 + half]), 1,
        )

    leaf_probes(0).start()
    loads[1].wait()
    loads[0].wait()

    def near_block(which, column):
        return near_v[pl.ds(2 * column + which, ROWS, stride=8), :]

    def hand_over(half):
        own = probes_v[:, K * half : K * (half + 1)]
        for j in range(ROWS // K):
            handed[half, K * j : K * (j + 1), :] = product(near_block(1, j), own, (0, 0))

    def times(which, values):
        out = None
        for j in range(0, ROWS // K, 2):
            block = jnp.concatenate([near_block(which, j), near_block(which, j + 1)], axis=1)
            part = product(block, values[K * j : K * (j + 2)])
            out = part if out is None else out + part
        return out

    def far_half(half, first_wait):
        lanes = slice(K * half, K * (half + 1))
        part = samples_v[:, lanes] - times(0, probes_v[:, lanes])
        leaf_probes(half).wait_recv()
        last = mine == total - 1
        upper = jnp.where(last, 0.0, next_probes[half])
        part = part - times(1, upper)
        leaf_handed(half).wait_recv()
        return part - jnp.where(mine == 0, 0.0, handed_in[half])

    hand_over(0)
    leaf_handed(0).start()
    leaf_probes(1).start()
    loads[2].wait()
    far1[...] = far_half(0, None)
    own1 = probes_v[:, :K]
    gram[:, :K] = product(far1[...], far1[...], (0, 0))
    gram[:, K:] = product(far1[...], own1, (0, 0))
    hand_over(1)
    leaf_handed(1).start()
    loads[3].wait()

    def stage(s):
        distance = 1 << s if isinstance(s, int) else lax.shift_left(jnp.int32(1), s)
        parity = lax.rem(lax.shift_right_logical(member, jnp.int32(s)), 2)
        lower = parity == 0
        node = lax.shift_right_logical(mine, jnp.int32(s))
        nodes = lax.shift_right_logical(jnp.int32(total), jnp.int32(s))

        def exchange(kind, t):
            d = 1 << t if isinstance(t, int) else lax.shift_left(jnp.int32(1), t)
            par = lax.rem(lax.shift_right_logical(member, jnp.int32(t)), 2)
            sibling = d * (1 - 2 * par)
            source, target, offset = {
                0: (w1_out, w1_in.at[0], 2 * d), 1: (w1_out, w1_in.at[1], -2 * d), 2: (w1_out, sib_in.at[0], sibling),
                3: (w2_out, w2_in.at[0], 2 * d), 4: (w2_out, w2_in.at[1], -2 * d), 5: (w2_out, sib_in.at[1], sibling),
                6: (e1_out, sib_in.at[2], sibling), 7: (e2_out, sib_in.at[3], sibling),
            }[kind]
            return send(source.at[t], target.at[t], (send_sem.at[kind, t], recv_sem.at[kind, t]), offset)

        def coupling_sides(t):
            par = lax.rem(lax.shift_right_logical(member, jnp.int32(t)), 2)
            per = lax.shift_right_logical(jnp.int32(leaves), jnp.int32(t))
            index = leaves - per + lax.shift_right_logical(member, jnp.int32(t + 1))
            own = couplings_v[slots[index], par]
            turned = own.T
            even = par == 0
            return jnp.where(even, own, turned), jnp.where(even, turned, own)

        def correct(z, incoming, t):
            q = lax.shift_right_logical(mine, jnp.int32(t))
            count = lax.shift_right_logical(jnp.int32(total), jnp.int32(t))
            from_left, from_right = coupling_sides(t)
            left = jnp.where(q >= 2, incoming[0, t], 0.0)
            right = jnp.where(q < count - 2, incoming[1, t], 0.0)
            sides = jnp.concatenate([from_left, from_right], axis=1)
            return z - product(sides, jnp.concatenate([left, right], axis=0))

        def stacked(own, sibling, t):
            par = lax.rem(lax.shift_right_logical(member, jnp.int32(t)), 2)
            even = par == 0
            return jnp.concatenate([jnp.where(even, own, sibling), jnp.where(even, sibling, own)], axis=0)

        def leaf_second():
            far2 = far_half(1, None)
            second[:, :K] = product(far1[...], far2, (0, 0))
            second[:, K:] = product(far1[...], probes_v[:, K:], (0, 0))

        def level_second():
            t = s - 1
            exchange(3, t).wait_recv()
            exchange(4, t).wait_recv()
            e2_out[t] = correct(z2[...], w2_in, t)
            exchange(7, t).start()

        def level_second_end():
            t = s - 1
            exchange(5, t).wait_recv()
            exchange(7, t).wait_recv()
            second[:, :K] = product(stack1[...], stacked(e2_out[t], sib_in[3, t], t), (0, 0))
            second[:, K:] = product(stack1[...], stacked(w2_out[t], sib_in[1, t], t), (0, 0))

        def middle():
            when(s == 0, leaf_second)
            when(s > 0, level_second)

        inverse[...] = inverse_factor(gram[:, :K], {8: middle})
        x = inverse[...]

        def forward():
            w1_out[s] = product(x, gram[:, K:])
            for kind in range(3):
                exchange(kind, s).start()

        when(s < levels, forward)
        when(s > 0, level_second_end)

        z1 = product(x, gram[:, :K])
        zw2 = product(x, second[...])

        def leaf_basis():
            q_leaf[...] = product(far1[...], x, (1, 1))
            pltpu.make_async_copy(q_leaf, leaf_out, out_sem.at[levels]).start()

        def level_basis():
            t = s - 1
            q_top[t] = product(stack1[...], x, (1, 1))
            pltpu.make_async_copy(q_top.at[t], transfer_out.at[t], out_sem.at[t]).start()

        def go_on():
            z2[...] = zw2[:, :K]
            w2_out[s] = zw2[:, K:]
            when(s == 0, leaf_basis)
            when(s > 0, level_basis)
            exchange(0, s).wait_recv()
            exchange(1, s).wait_recv()
            e1_out[s] = correct(z1, w1_in, s)
            exchange(6, s).start()
            for kind in range(3, 6):
                exchange(kind, s).start()
            exchange(2, s).wait_recv()
            exchange(6, s).wait_recv()
            stack = stacked(e1_out[s], sib_in[2, s], s)
            stack1[...] = stack
            gram[:, :K] = product(stack, stack, (0, 0))
            gram[:, K:] = product(stack, stacked(w1_out[s], sib_in[0, s], s), (0, 0))

        def finish():
            top_samples[:, :K] = z1
            top_samples[:, K:] = zw2[:, :K]
            top_probes[:, :K] = product(x, gram[:, K:])
            top_probes[:, K:] = zw2[:, K:]
            level_basis()

        when(s < levels, go_on)
        when(s == levels, finish)
        return exchange

    if UNROLL:
        for s in range(levels + 1):
            exchange = stage(s)
    else:
        def step(s, carry):
            stage(s)
            return carry
        lax.fori_loop(0, levels + 1, step, 0)

    for half in range(2):
        leaf_probes(half).wait_send()
        leaf_handed(half).wait_send()
    for t in range(levels):
        sources = [w1_out] * 3 + [w2_out] * 3 + [e1_out, e2_out]
        for kind, source in enumerate(sources):
            send(source.at[t], source.at[t], (send_sem.at[kind, t], recv_sem.at[kind, t]), 1).wait_send()
        pltpu.make_async_copy(q_top.at[t], transfer_out.at[t], out_sem.at[t]).wait()
    pltpu.make_async_copy(q_leaf, leaf_out, out_sem.at[levels]).wait()


UNROLL = False


def solution(mesh):
    leaves, subtrees = mesh.shape["leaf"], mesh.shape["clusters"]
    levels = leaves.bit_length() - 1

    def body(samples, probes, near_blocks, couplings, node_slot):
        near = near_blocks.reshape(ROWS, 2, ROWS // K, K).transpose(0, 2, 1, 3).reshape(-1, K)
        anywhere = pl.BlockSpec(memory_space=pl.ANY)
        vmem = pl.BlockSpec(memory_space=pltpu.VMEM)
        leaf_basis, transfer, top_samples, top_probes = pl.pallas_call(
            functools.partial(kernel, leaves, subtrees),
            out_shape=(
                jax.ShapeDtypeStruct((ROWS, K), f32),
                jax.ShapeDtypeStruct((levels, 2 * K, K), f32),
                jax.ShapeDtypeStruct((K, 2 * K), f32),
                jax.ShapeDtypeStruct((K, 2 * K), f32),
            ),
            in_specs=[pl.BlockSpec(memory_space=pltpu.SMEM)] + [anywhere] * 4,
            out_specs=(anywhere, anywhere, vmem, vmem),
            scratch_shapes=[
                pltpu.VMEM((8 * ROWS, K), f32),
                pltpu.VMEM((ROWS, 2 * K), f32),
                pltpu.VMEM((ROWS, 2 * K), f32),
                pltpu.VMEM(couplings.shape[1:], f32),
                pltpu.VMEM((2, ROWS, K), f32),
                pltpu.VMEM((2, ROWS, K), f32),
                pltpu.VMEM((2, ROWS, K), f32),
                pltpu.VMEM((ROWS, K), f32),
                pltpu.VMEM((K, 2 * K), f32),
                pltpu.VMEM((K, K), f32),
                pltpu.VMEM((K, 2 * K), f32),
                pltpu.VMEM((2 * K, K), f32),
                pltpu.VMEM((2 * K, K), f32),
                pltpu.VMEM((K, K), f32),
                pltpu.VMEM((2 * K, K), f32),
                pltpu.VMEM((2 * K, K), f32),
                pltpu.VMEM((levels, K, K), f32),
                pltpu.VMEM((levels, K, K), f32),
                pltpu.VMEM((levels, K, K), f32),
                pltpu.VMEM((levels, K, K), f32),
                pltpu.VMEM((2, levels, K, K), f32),
                pltpu.VMEM((2, levels, K, K), f32),
                pltpu.VMEM((4, levels, K, K), f32),
                pltpu.VMEM((ROWS, K), f32),
                pltpu.VMEM((levels, 2 * K, K), f32),
                pltpu.SemaphoreType.DMA((4,)),
                pltpu.SemaphoreType.DMA((4,)),
                pltpu.SemaphoreType.DMA((4,)),
                pltpu.SemaphoreType.DMA((8, levels)),
                pltpu.SemaphoreType.DMA((8, levels)),
                pltpu.SemaphoreType.DMA((levels + 1,)),
            ],
            compiler_params=pltpu.CompilerParams(
                collective_id=0, has_side_effects=True, vmem_limit_bytes=60 * 2**20
            ),
            name="nested_bases",
        )(node_slot[0], samples, probes, near, couplings[0])
        return leaf_basis, transfer[None], top_samples[None], top_probes[None]

    in_specs = (
        P(("clusters", "leaf"), None),
        P(("clusters", "leaf"), None),
        P(("clusters", "leaf"), None, None),
        P("clusters", None, None, None, None),
        P("clusters", None),
    )
    out_specs = (
        P(("clusters", "leaf"), None),
        P(("clusters", "leaf"), None, None, None),
        P("clusters", None, None),
        P("clusters", None, None),
    )
    return jax.shard_map(body, mesh=mesh, in_specs=in_specs, out_specs=out_specs, check_vma=False)
```

```python
import functools

import jax
import jax.numpy as jnp
from jax import lax
from jax.experimental import pallas as pl
from jax.experimental.pallas import tpu as pltpu
from jax.sharding import PartitionSpec as P

MESH = pl.DeviceIdType.MESH
f32 = jnp.float32
bf16 = jnp.bfloat16

K = 128
ROWS = 512
BLOCK = 8
REACH = 3


def halves(value):
    high = value.astype(bf16)
    return high, (value - high.astype(f32)).astype(bf16)


def product(a, b, contract=(1, 0)):
    dims = (((contract[0],), (contract[1],)), ((), ()))
    a_high, a_low = halves(a)
    b_high, b_low = halves(b)
    dot = functools.partial(lax.dot_general, dimension_numbers=dims, preferred_element_type=f32)
    return dot(a_high, b_high) + (dot(a_high, b_low) + dot(a_low, b_high))


def spread(block, column):
    return jnp.broadcast_to(block[:, column : column + 1], (block.shape[0], K))


def inverse_factor(gram, interludes):
    panels = K // BLOCK
    lane = lax.broadcasted_iota(jnp.int32, (BLOCK, K), 1)
    sub = lax.broadcasted_iota(jnp.int32, (BLOCK, K), 0)
    rounded = lambda v: v.astype(bf16).astype(f32)
    rows = [gram[BLOCK * g : BLOCK * (g + 1)] for g in range(panels)]
    pivot = [spread(rows[0], i) for i in range(BLOCK)]
    done = []
    for k in range(panels):
        if k in interludes:
            interludes[k]()
        first, after = BLOCK * k, BLOCK * (k + 1)
        near_end = min(panels, k + 1 + REACH)
        inside = (lane >= first) & (lane < after)
        panel = jnp.where(inside, (lane == first + sub).astype(f32), rows[k])
        below = coming = upcoming = far = None
        if k + 1 < panels:
            below = [spread(rows[k + 1], first + i) for i in range(BLOCK)]
            coming = [spread(rows[k + 1], after + i) for i in range(BLOCK)]
            upcoming = jnp.where(inside, 0.0, rows[k + 1])
        if near_end > k + 2:
            block = jnp.concatenate(rows[k + 2 : near_end], axis=0)
            far = [spread(block, first + i) for i in range(BLOCK)]
            wide = lax.broadcasted_iota(jnp.int32, block.shape, 1)
            far_rows = jnp.where((wide >= first) & (wide < after), 0.0, block)
        for i in range(BLOCK):
            scale = lax.rsqrt(pivot[i][i : i + 1, :])
            column = pivot[i] * scale
            row = panel[i : i + 1, :] * scale
            entry = [column[j : j + 1, :] for j in range(BLOCK)]
            for j in range(i + 1, BLOCK):
                pivot[j] = pivot[j] - column * entry[j]
            panel = jnp.where(sub == i, row, panel - jnp.where(sub > i, column, 0.0) * row)
            if below is not None:
                lower = below[i] * scale
                for j in range(i + 1, BLOCK):
                    below[j] = below[j] - lower * entry[j]
                for j in range(BLOCK):
                    coming[j] = coming[j] - lower * lower[j : j + 1, :]
                upcoming = upcoming - lower * row
            if far is not None:
                lowest = far[i] * scale
                for j in range(i + 1, BLOCK):
                    far[j] = far[j] - lowest * entry[j]
                far_rows = far_rows - lowest * row
        done.append(jnp.where(lane < after, panel, 0.0))
        pivot = coming
        if below is not None:
            rows[k + 1] = upcoming
        if far is not None:
            for g in range(k + 2, near_end):
                rows[g] = far_rows[BLOCK * (g - k - 2) : BLOCK * (g - k - 1)]
        if near_end < panels:
            high = rounded(panel)
            middle = rounded(panel - high)
            low = rounded(panel - high - middle)
            left = jnp.concatenate([high, high, middle, high, low, middle], axis=0).astype(bf16)
            right = jnp.concatenate([high, middle, high, low, high, middle], axis=0).astype(bf16)
            update = lax.dot_general(
                left, right, (((0,), (0,)), ((), ())), preferred_element_type=f32
            )
            for g in range(near_end, panels):
                rows[g] = jnp.where(inside, 0.0, rows[g]) - update[BLOCK * g : BLOCK * (g + 1)]
    return jnp.concatenate(done, axis=0)


GROUPS = 3


def kernel(
    leaves, subtrees, slots, samples, probes, near, couplings,
    leaf_out, transfer_out, top_samples, top_probes,
    near_v, probes_v, samples_v, couplings_v, next_probes, handed, handed_in, far1,
    gram, inverse, inner, sent, far_in, corrected, passed, gathered, q_leaf, q_top,
    local_sem, leaf_send, leaf_recv, far_send, far_recv, pass_send, pass_recv,
    join_send, join_recv, last_send, last_recv, out_sem,
):
    levels = leaves.bit_length() - 1
    total = leaves * subtrees
    member = lax.axis_index("leaf")
    cluster = lax.axis_index("clusters")
    mine = cluster * leaves + member

    def along(offset):
        index = lax.rem(mine + offset + total, total)
        return {"leaf": lax.rem(index, leaves), "clusters": index // leaves}

    def across(mask):
        return {"leaf": jnp.bitwise_xor(member, mask), "clusters": cluster}

    def send(source, target, sems, device):
        return pltpu.make_async_remote_copy(
            src_ref=source, dst_ref=target, send_sem=sems[0], recv_sem=sems[1],
            device_id=device, device_id_type=MESH,
        )

    def bit(i):
        return lax.rem(lax.shift_right_logical(member, jnp.int32(i)), 2)

    def width(t):
        return K >> t

    def begin(t):
        start = jnp.int32(0)
        for i in range(t):
            start = start + bit(i) * (K >> (i + 1))
        return pl.multiple_of(start, BLOCK)

    barrier = pltpu.get_barrier_semaphore()
    peers = [along(side << i) for i in range(levels + 1) for side in (1, -1)]
    peers += [across(mask) for mask in range(1, leaves)]
    for peer in peers:
        pl.semaphore_signal(barrier, inc=1, device_id=peer, device_id_type=MESH)

    loads = [
        pltpu.make_async_copy(near, near_v, local_sem.at[0]),
        pltpu.make_async_copy(probes, probes_v, local_sem.at[1]),
        pltpu.make_async_copy(samples, samples_v, local_sem.at[2]),
        pltpu.make_async_copy(couplings, couplings_v, local_sem.at[3]),
    ]
    for load in loads:
        load.start()

    def leaf_probes(half):
        return send(
            probes.at[:, K * half : K * (half + 1)], next_probes.at[half],
            (leaf_send.at[half], leaf_recv.at[half]), along(-1),
        )

    def leaf_handed(half):
        return send(
            handed.at[half], handed_in.at[half],
            (leaf_send.at[2 + half], leaf_recv.at[2 + half]), along(1),
        )

    def near_block(which, column):
        return near_v[pl.ds(2 * column + which, ROWS, stride=8), :]

    def times(which, values):
        out = None
        for j in range(0, ROWS // K, 2):
            block = jnp.concatenate([near_block(which, j), near_block(which, j + 1)], axis=1)
            part = product(block, values[K * j : K * (j + 2)])
            out = part if out is None else out + part
        return out

    loads[0].wait()
    loads[1].wait()
    for j in range(ROWS // K):
        block = product(near_block(1, j), probes_v[...], (0, 0))
        handed[0, K * j : K * (j + 1), :] = block[:, :K]
        handed[1, K * j : K * (j + 1), :] = block[:, K:]
    loads[2].wait()
    samples_v[...] = samples_v[...] - times(0, probes_v[...])

    pl.semaphore_wait(barrier, len(peers))
    for half in range(2):
        leaf_handed(half).start()
        leaf_probes(half).start()
    def far_half(half):
        leaf_probes(half).wait_recv()
        upper = jnp.where(mine == total - 1, 0.0, next_probes[half])
        part = samples_v[:, K * half : K * (half + 1)] - times(1, upper)
        leaf_handed(half).wait_recv()
        return part - jnp.where(mine == 0, 0.0, handed_in[half])

    far1[...] = far_half(0)
    gram[...] = product(far1[...], far1[...], (0, 0))

    def far_copy(t, group, side):
        n = width(t)
        return send(
            sent.at[t, group, pl.ds(0, n)], far_in.at[side, t, group, pl.ds(0, n)],
            (far_send.at[side, t, group], far_recv.at[side, t, group]), along((2 << t) * (1 - 2 * side)),
        )

    def pass_copy(t):
        n = width(t) // 2
        away = pl.multiple_of((1 - bit(t)) * n, BLOCK)
        return send(
            sent.at[t, :, pl.ds(away, n)], passed.at[t, :, pl.ds(0, n)],
            (pass_send.at[t], pass_recv.at[t]), across(1 << t),
        )

    def join_copy(t, mask):
        part = corrected.at[t, bit(t), pl.ds(begin(t), width(t))]
        return send(part, part, (join_send.at[t, mask], join_recv.at[t, mask]), across(mask))

    def last_copy(mask):
        part = gathered.at[:, pl.ds(begin(levels), width(levels))]
        return send(part, part, (last_send.at[mask], last_recv.at[mask]), across(mask))

    def far_order(count):
        return sorted(range(1, count), key=lambda mask: -mask)

    def leaf_second():
        loads[3].wait()
        far2 = far_half(1)
        tall = jnp.concatenate([far2, probes_v[:, K:], probes_v[:, :K]], axis=1)
        block = product(tall, far1[...], (0, 0))
        for group in range(GROUPS):
            inner[group] = block[K * group : K * (group + 1)]

    def leaf_basis():
        q_leaf[...] = product(far1[...], inverse[...], (1, 1))
        pltpu.make_async_copy(q_leaf, leaf_out, out_sem.at[levels]).start()

    def level_basis(t):
        x = inverse[...]
        for child in range(2):
            q_top[t, K * child : K * (child + 1), :] = product(corrected[t, child], x, (0, 1))
        pltpu.make_async_copy(q_top.at[t], transfer_out.at[t], out_sem.at[t]).start()

    def merge(t):
        n = width(t)
        x = inverse[...]
        sent[t, 2, :n] = product(inner[2, :n], x, (1, 1))
        far_copy(t, 2, 0).start()
        far_copy(t, 2, 1).start()
        both = product(jnp.concatenate([inner[1, :n], inner[0, :n]], axis=0), x, (1, 1))
        sent[t, 1, :n] = both[:n]
        far_copy(t, 1, 0).start()
        far_copy(t, 1, 1).start()
        own = product(gram[pl.ds(begin(t), n)], x, (1, 1))
        per = leaves >> t
        index = leaves - per + lax.shift_right_logical(member, jnp.int32(t + 1))
        coupling = couplings_v[slots[index], bit(t)]
        turned = coupling.T
        even = bit(t) == 0
        sides = jnp.concatenate([jnp.where(even, coupling, turned), jnp.where(even, turned, coupling)], axis=1)
        node = lax.shift_right_logical(mine, jnp.int32(t))
        has_left, has_right = node >= 2, node < (total >> t) - 2
        if t == 0:
            leaf_basis()
        else:
            level_basis(t - 1)

        def correct(z, group):
            left = jnp.where(has_left, far_in[0, t, group, :n], 0.0)
            right = jnp.where(has_right, far_in[1, t, group, :n], 0.0)
            return z - product(jnp.concatenate([left, right], axis=1), sides, (1, 1))

        far_copy(t, 2, 0).wait_recv()
        far_copy(t, 2, 1).wait_recv()
        corrected[t, bit(t), pl.ds(begin(t), n)] = correct(own, 2)
        for mask in far_order(2 << t):
            join_copy(t, mask).start()
        far_copy(t, 1, 0).wait_recv()
        far_copy(t, 1, 1).wait_recv()
        sent[t, 0, :n] = correct(both[n:], 1)
        pass_copy(t).start()

        for mask in far_order(2 << t):
            join_copy(t, mask).wait_recv()
        wide = jnp.concatenate([corrected[t, 0], corrected[t, 1]], axis=1)
        gram[...] = product(wide, wide, (1, 1))
        pass_copy(t).wait_recv()
        h = n // 2
        keep = pl.multiple_of(bit(t) * h, BLOCK)
        kept = jnp.concatenate([sent[t, group, pl.ds(keep, h)] for group in range(GROUPS)], axis=0)
        came = jnp.concatenate([passed[t, group, :h] for group in range(GROUPS)], axis=0)
        pair = jnp.concatenate([jnp.where(even, kept, came), jnp.where(even, came, kept)], axis=1)
        block = product(pair, wide, (1, 1))
        if t + 1 < levels:
            for group in range(GROUPS):
                inner[group, :h] = block[h * group : h * (group + 1)]
        else:
            for group in range(GROUPS):
                gathered[group, pl.ds(begin(levels), h)] = block[h * group : h * (group + 1)]
            for mask in far_order(leaves):
                last_copy(mask).start()

    def finish():
        x = inverse[...]
        level_basis(levels - 1)
        top_samples[:, :K] = product(x, gram[...], (1, 1))
        for mask in far_order(leaves):
            last_copy(mask).wait_recv()
        block = product(x, jnp.concatenate([gathered[group] for group in range(GROUPS)], axis=0), (1, 1))
        top_samples[:, K:] = block[:, :K]
        top_probes[:, K:] = block[:, K : 2 * K]
        top_probes[:, :K] = block[:, 2 * K :]

    def step(s, carry):
        inverse[...] = inverse_factor(gram[...], {8: lambda: pl.when(s == 0)(leaf_second)})
        for t in range(levels):
            pl.when(s == t)(functools.partial(merge, t))
        pl.when(s == levels)(finish)
        return carry

    lax.fori_loop(0, levels + 1, step, 0)

    for half in range(2):
        leaf_probes(half).wait_send()
        leaf_handed(half).wait_send()
    for t in range(levels):
        for group in (2, 1):
            for side in range(2):
                far_copy(t, group, side).wait_send()
        pass_copy(t).wait_send()
        for mask in far_order(2 << t):
            join_copy(t, mask).wait_send()
        pltpu.make_async_copy(q_top.at[t], transfer_out.at[t], out_sem.at[t]).wait()
    for mask in far_order(leaves):
        last_copy(mask).wait_send()
    pltpu.make_async_copy(q_leaf, leaf_out, out_sem.at[levels]).wait()


def hand_out(*refs):
    count = len(refs) // 2
    for i in range(count):
        refs[count + i][...] = refs[i][...]


def solution(mesh):
    leaves, subtrees = mesh.shape["leaf"], mesh.shape["clusters"]
    levels = leaves.bit_length() - 1

    def body(samples, probes, near_blocks, couplings, node_slot):
        near = near_blocks.reshape(ROWS, 2, ROWS // K, K).transpose(0, 2, 1, 3).reshape(-1, K)
        anywhere = pl.BlockSpec(memory_space=pl.ANY)
        vmem = pl.BlockSpec(memory_space=pltpu.VMEM)
        shapes = (
            jax.ShapeDtypeStruct((ROWS, K), f32),
            jax.ShapeDtypeStruct((levels, 2 * K, K), f32),
            jax.ShapeDtypeStruct((K, 2 * K), f32),
            jax.ShapeDtypeStruct((K, 2 * K), f32),
        )
        dma = pltpu.SemaphoreType.DMA
        results = pl.pallas_call(
            functools.partial(kernel, leaves, subtrees),
            out_shape=shapes,
            in_specs=[pl.BlockSpec(memory_space=pltpu.SMEM)] + [anywhere] * 4,
            out_specs=(anywhere, anywhere, vmem, vmem),
            scratch_shapes=[
                pltpu.VMEM((8 * ROWS, K), f32),
                pltpu.VMEM((ROWS, 2 * K), f32),
                pltpu.VMEM((ROWS, 2 * K), f32),
                pltpu.VMEM(couplings.shape[1:], f32),
                pltpu.VMEM((2, ROWS, K), f32),
                pltpu.VMEM((2, ROWS, K), f32),
                pltpu.VMEM((2, ROWS, K), f32),
                pltpu.VMEM((ROWS, K), f32),
                pltpu.VMEM((K, K), f32),
                pltpu.VMEM((K, K), f32),
                pltpu.VMEM((GROUPS, K, K), f32),
                pltpu.VMEM((levels, GROUPS, K, K), f32),
                pltpu.VMEM((2, levels, GROUPS, K, K), f32),
                pltpu.VMEM((levels, 2, K, K), f32),
                pltpu.VMEM((levels, GROUPS, K // 2, K), f32),
                pltpu.VMEM((GROUPS, K, K), f32),
                pltpu.VMEM((ROWS, K), f32),
                pltpu.VMEM((levels, 2 * K, K), f32),
                dma((4,)), dma((4,)), dma((4,)),
                dma((2, levels, GROUPS)), dma((2, levels, GROUPS)),
                dma((levels,)), dma((levels,)),
                dma((levels, leaves)), dma((levels, leaves)),
                dma((leaves,)), dma((leaves,)),
                dma((levels + 1,)),
            ],
            compiler_params=pltpu.CompilerParams(
                collective_id=0, has_side_effects=True, vmem_limit_bytes=60 * 2**20
            ),
            name="nested_bases",
        )(node_slot[0], samples, probes, near, couplings[0])
        leaf_basis, transfer, top_samples, top_probes = pl.pallas_call(
            hand_out,
            out_shape=shapes,
            in_specs=[vmem] * 4,
            out_specs=(vmem,) * 4,
            name="hand_out",
        )(*results)
        return leaf_basis, transfer[None], top_samples[None], top_probes[None]

    in_specs = (
        P(("clusters", "leaf"), None),
        P(("clusters", "leaf"), None),
        P(("clusters", "leaf"), None, None),
        P("clusters", None, None, None, None),
        P("clusters", None),
    )
    out_specs = (
        P(("clusters", "leaf"), None),
        P(("clusters", "leaf"), None, None, None),
        P("clusters", None, None),
        P("clusters", None, None),
    )
    return jax.shard_map(body, mesh=mesh, in_specs=in_specs, out_specs=out_specs, check_vma=False)
```

```python
import functools

import jax
import jax.numpy as jnp
from jax import lax
from jax.experimental import pallas as pl
from jax.experimental.pallas import tpu as pltpu
from jax.sharding import PartitionSpec as P

MESH = pl.DeviceIdType.MESH
f32 = jnp.float32
bf16 = jnp.bfloat16

K = 128
ROWS = 512
BLOCK = 8
REACH = 3


def halves(value):
    high = value.astype(bf16)
    return high, (value - high.astype(f32)).astype(bf16)


def product(a, b, contract=(1, 0)):
    dims = (((contract[0],), (contract[1],)), ((), ()))
    a_high, a_low = halves(a)
    b_high, b_low = halves(b)
    dot = functools.partial(lax.dot_general, dimension_numbers=dims, preferred_element_type=f32)
    return dot(a_high, b_high) + (dot(a_high, b_low) + dot(a_low, b_high))


def spread(block, column):
    return jnp.broadcast_to(block[:, column : column + 1], (block.shape[0], K))


def inverse_factor(gram, interludes):
    panels = K // BLOCK
    lane = lax.broadcasted_iota(jnp.int32, (BLOCK, K), 1)
    sub = lax.broadcasted_iota(jnp.int32, (BLOCK, K), 0)
    rounded = lambda v: v.astype(bf16).astype(f32)
    rows = [gram[BLOCK * g : BLOCK * (g + 1)] for g in range(panels)]
    pivot = [spread(rows[0], i) for i in range(BLOCK)]
    done = []
    for k in range(panels):
        if k in interludes:
            interludes[k]()
        first, after = BLOCK * k, BLOCK * (k + 1)
        near_end = min(panels, k + 1 + REACH)
        inside = (lane >= first) & (lane < after)
        panel = jnp.where(inside, (lane == first + sub).astype(f32), rows[k])
        below = coming = upcoming = far = None
        if k + 1 < panels:
            below = [spread(rows[k + 1], first + i) for i in range(BLOCK)]
            coming = [spread(rows[k + 1], after + i) for i in range(BLOCK)]
            upcoming = jnp.where(inside, 0.0, rows[k + 1])
        if near_end > k + 2:
            block = jnp.concatenate(rows[k + 2 : near_end], axis=0)
            far = [spread(block, first + i) for i in range(BLOCK)]
            wide = lax.broadcasted_iota(jnp.int32, block.shape, 1)
            far_rows = jnp.where((wide >= first) & (wide < after), 0.0, block)
        for i in range(BLOCK):
            scale = lax.rsqrt(pivot[i][i : i + 1, :])
            column = pivot[i] * scale
            row = panel[i : i + 1, :] * scale
            entry = [column[j : j + 1, :] for j in range(BLOCK)]
            for j in range(i + 1, BLOCK):
                pivot[j] = pivot[j] - column * entry[j]
            panel = jnp.where(sub == i, row, panel - jnp.where(sub > i, column, 0.0) * row)
            if below is not None:
                lower = below[i] * scale
                for j in range(i + 1, BLOCK):
                    below[j] = below[j] - lower * entry[j]
                for j in range(BLOCK):
                    coming[j] = coming[j] - lower * lower[j : j + 1, :]
                upcoming = upcoming - lower * row
            if far is not None:
                lowest = far[i] * scale
                for j in range(i + 1, BLOCK):
                    far[j] = far[j] - lowest * entry[j]
                far_rows = far_rows - lowest * row
        done.append(jnp.where(lane < after, panel, 0.0))
        pivot = coming
        if below is not None:
            rows[k + 1] = upcoming
        if far is not None:
            for g in range(k + 2, near_end):
                rows[g] = far_rows[BLOCK * (g - k - 2) : BLOCK * (g - k - 1)]
        if near_end < panels:
            high = rounded(panel)
            middle = rounded(panel - high)
            low = rounded(panel - high - middle)
            left = jnp.concatenate([high, high, middle, high, low, middle], axis=0).astype(bf16)
            right = jnp.concatenate([high, middle, high, low, high, middle], axis=0).astype(bf16)
            update = lax.dot_general(
                left, right, (((0,), (0,)), ((), ())), preferred_element_type=f32
            )
            for g in range(near_end, panels):
                rows[g] = jnp.where(inside, 0.0, rows[g]) - update[BLOCK * g : BLOCK * (g + 1)]
    return jnp.concatenate(done, axis=0)


NEAR_PARTS = 4
GROUPS = 3


def kernel(
    leaves, subtrees, slots, samples, probes, near, couplings,
    leaf_out, transfer_out, top_samples, top_probes,
    near_v, probes_v, samples_v, couplings_v, next_probes, handed, handed_in, far1,
    gram, inverse, inner, sent, far_in, corrected, passed, gathered, q_leaf, q_top,
    local_sem, leaf_send, leaf_recv, far_send, far_recv, pass_send, pass_recv,
    join_send, join_recv, last_send, last_recv, out_sem,
):
    levels = leaves.bit_length() - 1
    total = leaves * subtrees
    member = lax.axis_index("leaf")
    cluster = lax.axis_index("clusters")
    mine = cluster * leaves + member

    def along(offset):
        index = lax.rem(mine + offset + total, total)
        return {"leaf": lax.rem(index, leaves), "clusters": index // leaves}

    def across(mask):
        return {"leaf": jnp.bitwise_xor(member, mask), "clusters": cluster}

    def send(source, target, sems, device):
        return pltpu.make_async_remote_copy(
            src_ref=source, dst_ref=target, send_sem=sems[0], recv_sem=sems[1],
            device_id=device, device_id_type=MESH,
        )

    def bit(i):
        return lax.rem(lax.shift_right_logical(member, jnp.int32(i)), 2)

    def share(i):
        return jnp.bitwise_xor(bit(1), bit(3)) if i == 1 and levels > 3 else bit(i)

    def width(t):
        return K >> t

    def begin(t):
        start = jnp.int32(0)
        for i in range(t):
            start = start + share(i) * (K >> (i + 1))
        return pl.multiple_of(start, BLOCK)

    barrier = pltpu.get_barrier_semaphore()
    peers = [along(1), along(-1)]
    for peer in peers:
        pl.semaphore_signal(barrier, inc=1, device_id=peer, device_id_type=MESH)

    fetch_probes = pltpu.make_async_copy(probes, probes_v, local_sem.at[0])
    fetch_samples = pltpu.make_async_copy(samples, samples_v, local_sem.at[1])
    fetch_couplings = pltpu.make_async_copy(couplings, couplings_v, local_sem.at[2])
    fetch_near = []
    for i in range(NEAR_PARTS):
        part = pl.ds(i * (8 * ROWS // NEAR_PARTS), 8 * ROWS // NEAR_PARTS)
        fetch_near.append(pltpu.make_async_copy(near.at[part], near_v.at[part], local_sem.at[3 + i]))
    fetch_probes.start()
    for fetch in fetch_near:
        fetch.start()
    fetch_samples.start()

    def leaf_probes(half):
        return send(
            probes.at[:, K * half : K * (half + 1)], next_probes.at[half],
            (leaf_send.at[half], leaf_recv.at[half]), along(-1),
        )

    def leaf_handed(half):
        return send(
            handed.at[half], handed_in.at[half],
            (leaf_send.at[2 + half], leaf_recv.at[2 + half]), along(1),
        )

    def near_block(which, column):
        return near_v[pl.ds(2 * column + which, ROWS, stride=8), :]

    def times(which, values):
        out = None
        for j in range(0, ROWS // K, 2):
            block = jnp.concatenate([near_block(which, j), near_block(which, j + 1)], axis=1)
            part = product(block, values[K * j : K * (j + 2)])
            out = part if out is None else out + part
        return out

    fetch_probes.wait()
    for fetch in fetch_near:
        fetch.wait()
    fetch_couplings.start()
    pl.semaphore_wait(barrier, len(peers))
    leaf_probes(0).start()
    for j in range(ROWS // K):
        block = product(near_block(1, j), probes_v[...], (0, 0))
        handed[0, K * j : K * (j + 1), :] = block[:, :K]
        handed[1, K * j : K * (j + 1), :] = block[:, K:]
    leaf_handed(0).start()
    leaf_probes(1).start()
    leaf_handed(1).start()
    fetch_samples.wait()
    samples_v[...] = samples_v[...] - times(0, probes_v[...])
    def far_half(half):
        leaf_probes(half).wait_recv()
        upper = jnp.where(mine == total - 1, 0.0, next_probes[half])
        part = samples_v[:, K * half : K * (half + 1)] - times(1, upper)
        leaf_handed(half).wait_recv()
        return part - jnp.where(mine == 0, 0.0, handed_in[half])

    far1[...] = far_half(0)
    gram[...] = product(far1[...], far1[...], (0, 0))

    def far_copy(t, group, side):
        n = width(t)
        device = along((2 << t) * (1 - 2 * side))
        if t == 2 and levels > 3:
            device["leaf"] = jnp.bitwise_xor(device["leaf"], 2)
        return send(
            sent.at[t, group, pl.ds(0, n)], far_in.at[side, t, group, pl.ds(0, n)],
            (far_send.at[side, t, group], far_recv.at[side, t, group]), device,
        )

    def pass_copy(t):
        n = width(t) // 2
        away = pl.multiple_of((1 - share(t)) * n, BLOCK)
        return send(
            sent.at[t, :, pl.ds(away, n)], passed.at[t, :, pl.ds(0, n)],
            (pass_send.at[t], pass_recv.at[t]), across(1 << t),
        )

    def join_copy(t, mask):
        part = corrected.at[t, bit(t), pl.ds(begin(t), width(t))]
        return send(part, part, (join_send.at[t, mask], join_recv.at[t, mask]), across(mask))

    top = levels - 1

    def last_copy(first, count, mask):
        part = gathered.at[pl.ds(first, count), bit(top), pl.ds(begin(top), width(top))]
        return send(part, part, (last_send.at[first, mask], last_recv.at[first, mask]), across(mask))

    def far_order(count):
        return sorted(range(1, count), key=lambda mask: -mask)

    def leaf_second():
        fetch_couplings.wait()
        far2 = far_half(1)
        tall = jnp.concatenate([far2, probes_v[:, K:], probes_v[:, :K]], axis=1)
        block = product(tall, far1[...], (0, 0))
        for group in range(GROUPS):
            inner[group] = block[K * group : K * (group + 1)]

    def leaf_basis():
        q_leaf[...] = product(far1[...], inverse[...], (1, 1))
        pltpu.make_async_copy(q_leaf, leaf_out, out_sem.at[levels]).start()

    def level_basis(t):
        x = inverse[...]
        for child in range(2):
            q_top[t, K * child : K * (child + 1), :] = product(corrected[t, child], x, (0, 1))
        pltpu.make_async_copy(q_top.at[t], transfer_out.at[t], out_sem.at[t]).start()

    def merge(t):
        n = width(t)
        x = inverse[...]
        sent[t, 2, :n] = product(inner[2, :n], x, (1, 1))
        far_copy(t, 2, 0).start()
        far_copy(t, 2, 1).start()
        both = product(jnp.concatenate([inner[1, :n], inner[0, :n]], axis=0), x, (1, 1))
        sent[t, 1, :n] = both[:n]
        far_copy(t, 1, 0).start()
        far_copy(t, 1, 1).start()
        if t == top:
            for group in (1, 2):
                gathered[group, bit(t), pl.ds(begin(t), n)] = sent[t, group, :n]
            for mask in far_order(leaves):
                last_copy(1, 2, mask).start()
        own = product(gram[pl.ds(begin(t), n)], x, (1, 1))
        per = leaves >> t
        index = leaves - per + lax.shift_right_logical(member, jnp.int32(t + 1))
        coupling = couplings_v[slots[index], bit(t)]
        turned = coupling.T
        even = bit(t) == 0
        sides = jnp.concatenate([jnp.where(even, coupling, turned), jnp.where(even, turned, coupling)], axis=1)
        node = lax.shift_right_logical(mine, jnp.int32(t))
        has_left, has_right = node >= 2, node < (total >> t) - 2
        if t == 0:
            leaf_basis()
        else:
            level_basis(t - 1)

        def correct(z, group):
            left = jnp.where(has_left, far_in[0, t, group, :n], 0.0)
            right = jnp.where(has_right, far_in[1, t, group, :n], 0.0)
            return z - product(jnp.concatenate([left, right], axis=1), sides, (1, 1))

        far_copy(t, 2, 0).wait_recv()
        far_copy(t, 2, 1).wait_recv()
        corrected[t, bit(t), pl.ds(begin(t), n)] = correct(own, 2)
        for mask in far_order(2 << t):
            join_copy(t, mask).start()
        far_copy(t, 1, 0).wait_recv()
        far_copy(t, 1, 1).wait_recv()
        second = correct(both[n:], 1)
        if t == top:
            gathered[0, bit(t), pl.ds(begin(t), n)] = second
            for mask in far_order(leaves):
                last_copy(0, 1, mask).start()
        else:
            sent[t, 0, :n] = second
            pass_copy(t).start()

        for mask in far_order(2 << t):
            join_copy(t, mask).wait_recv()
        wide = jnp.concatenate([corrected[t, 0], corrected[t, 1]], axis=1)
        gram[...] = product(wide, wide, (1, 1))
        if t == top:
            return
        pass_copy(t).wait_recv()
        h = n // 2
        keep = pl.multiple_of(share(t) * h, BLOCK)
        kept = jnp.concatenate([sent[t, group, pl.ds(keep, h)] for group in range(GROUPS)], axis=0)
        came = jnp.concatenate([passed[t, group, :h] for group in range(GROUPS)], axis=0)
        pair = jnp.concatenate([jnp.where(even, kept, came), jnp.where(even, came, kept)], axis=1)
        block = product(pair, wide, (1, 1))
        for group in range(GROUPS):
            inner[group, :h] = block[h * group : h * (group + 1)]

    def last_inner(first, count):
        for mask in far_order(leaves):
            last_copy(first, count, mask).wait_recv()
        wide = jnp.concatenate([corrected[top, 0], corrected[top, 1]], axis=1)
        for group in range(first, first + count):
            pair = jnp.concatenate([gathered[group, 0], gathered[group, 1]], axis=1)
            inner[group] = product(pair, wide, (1, 1))

    def finish():
        x = inverse[...]
        level_basis(levels - 1)
        top_samples[:, :K] = product(x, gram[...], (1, 1))
        last_inner(0, 1)
        block = product(x, jnp.concatenate([inner[group] for group in range(GROUPS)], axis=0), (1, 1))
        top_samples[:, K:] = block[:, :K]
        top_probes[:, K:] = block[:, K : 2 * K]
        top_probes[:, :K] = block[:, 2 * K :]

    def step(s, carry):
        def beside():
            pl.when(s == 0)(leaf_second)
            pl.when(s == levels)(functools.partial(last_inner, 1, 2))

        inverse[...] = inverse_factor(gram[...], {8: beside})
        for t in range(levels):
            pl.when(s == t)(functools.partial(merge, t))
        pl.when(s == levels)(finish)
        return carry

    lax.fori_loop(0, levels + 1, step, 0)

    for half in range(2):
        leaf_probes(half).wait_send()
        leaf_handed(half).wait_send()
    for t in range(levels):
        for group in (2, 1):
            for side in range(2):
                far_copy(t, group, side).wait_send()
        if t < top:
            pass_copy(t).wait_send()
        for mask in far_order(2 << t):
            join_copy(t, mask).wait_send()
        pltpu.make_async_copy(q_top.at[t], transfer_out.at[t], out_sem.at[t]).wait()
    for mask in far_order(leaves):
        last_copy(1, 2, mask).wait_send()
        last_copy(0, 1, mask).wait_send()
    pltpu.make_async_copy(q_leaf, leaf_out, out_sem.at[levels]).wait()


def hand_out(*refs):
    count = len(refs) // 2
    for i in range(count):
        refs[count + i][...] = refs[i][...]


def solution(mesh):
    leaves, subtrees = mesh.shape["leaf"], mesh.shape["clusters"]
    levels = leaves.bit_length() - 1

    def body(samples, probes, near_blocks, couplings, node_slot):
        near = near_blocks.reshape(ROWS, 2, ROWS // K, K).transpose(0, 2, 1, 3).reshape(-1, K)
        anywhere = pl.BlockSpec(memory_space=pl.ANY)
        vmem = pl.BlockSpec(memory_space=pltpu.VMEM)
        shapes = (
            jax.ShapeDtypeStruct((ROWS, K), f32),
            jax.ShapeDtypeStruct((levels, 2 * K, K), f32),
            jax.ShapeDtypeStruct((K, 2 * K), f32),
            jax.ShapeDtypeStruct((K, 2 * K), f32),
        )
        dma = pltpu.SemaphoreType.DMA
        results = pl.pallas_call(
            functools.partial(kernel, leaves, subtrees),
            out_shape=shapes,
            in_specs=[pl.BlockSpec(memory_space=pltpu.SMEM)] + [anywhere] * 4,
            out_specs=(anywhere, anywhere, vmem, vmem),
            scratch_shapes=[
                pltpu.VMEM((8 * ROWS, K), f32),
                pltpu.VMEM((ROWS, 2 * K), f32),
                pltpu.VMEM((ROWS, 2 * K), f32),
                pltpu.VMEM(couplings.shape[1:], f32),
                pltpu.VMEM((2, ROWS, K), f32),
                pltpu.VMEM((2, ROWS, K), f32),
                pltpu.VMEM((2, ROWS, K), f32),
                pltpu.VMEM((ROWS, K), f32),
                pltpu.VMEM((K, K), f32),
                pltpu.VMEM((K, K), f32),
                pltpu.VMEM((GROUPS, K, K), f32),
                pltpu.VMEM((levels, GROUPS, K, K), f32),
                pltpu.VMEM((2, levels, GROUPS, K, K), f32),
                pltpu.VMEM((levels, 2, K, K), f32),
                pltpu.VMEM((levels, GROUPS, K // 2, K), f32),
                pltpu.VMEM((GROUPS, 2, K, K), f32),
                pltpu.VMEM((ROWS, K), f32),
                pltpu.VMEM((levels, 2 * K, K), f32),
                dma((3 + NEAR_PARTS,)), dma((4,)), dma((4,)),
                dma((2, levels, GROUPS)), dma((2, levels, GROUPS)),
                dma((levels,)), dma((levels,)),
                dma((levels, leaves)), dma((levels, leaves)),
                dma((2, leaves)), dma((2, leaves)),
                dma((levels + 1,)),
            ],
            compiler_params=pltpu.CompilerParams(
                collective_id=0, has_side_effects=True, vmem_limit_bytes=60 * 2**20
            ),
            name="nested_bases",
        )(node_slot[0], samples, probes, near, couplings[0])
        leaf_basis, transfer, top_samples, top_probes = pl.pallas_call(
            hand_out,
            out_shape=shapes,
            in_specs=[vmem] * 4,
            out_specs=(vmem,) * 4,
            name="hand_out",
        )(*results)
        return leaf_basis, transfer[None], top_samples[None], top_probes[None]

    in_specs = (
        P(("clusters", "leaf"), None),
        P(("clusters", "leaf"), None),
        P(("clusters", "leaf"), None, None),
        P("clusters", None, None, None, None),
        P("clusters", None),
    )
    out_specs = (
        P(("clusters", "leaf"), None),
        P(("clusters", "leaf"), None, None, None),
        P("clusters", None, None),
        P("clusters", None, None),
    )
    return jax.shard_map(body, mesh=mesh, in_specs=in_specs, out_specs=out_specs, check_vma=False)
```

```python
import functools

import jax
import jax.numpy as jnp
from jax import lax
from jax.experimental import pallas as pl
from jax.experimental.pallas import tpu as pltpu
from jax.sharding import PartitionSpec as P

MESH = pl.DeviceIdType.MESH
f32 = jnp.float32
bf16 = jnp.bfloat16

K = 128
ROWS = 512
BLOCK = 8
REACH = 3


def halves(value):
    high = value.astype(bf16)
    return high, (value - high.astype(f32)).astype(bf16)


def product(a, b, contract=(1, 0)):
    dims = (((contract[0],), (contract[1],)), ((), ()))
    a_high, a_low = halves(a)
    b_high, b_low = halves(b)
    dot = functools.partial(lax.dot_general, dimension_numbers=dims, preferred_element_type=f32)
    return dot(a_high, b_high) + (dot(a_high, b_low) + dot(a_low, b_high))


def spread(block, column):
    return jnp.broadcast_to(block[:, column : column + 1], (block.shape[0], K))


def inverse_factor(gram, interludes):
    panels = K // BLOCK
    lane = lax.broadcasted_iota(jnp.int32, (BLOCK, K), 1)
    sub = lax.broadcasted_iota(jnp.int32, (BLOCK, K), 0)
    rounded = lambda v: v.astype(bf16).astype(f32)
    rows = [gram[BLOCK * g : BLOCK * (g + 1)] for g in range(panels)]
    pivot = [spread(rows[0], i) for i in range(BLOCK)]
    done = []
    for k in range(panels):
        if k in interludes:
            interludes[k]()
        first, after = BLOCK * k, BLOCK * (k + 1)
        near_end = min(panels, k + 1 + REACH)
        inside = (lane >= first) & (lane < after)
        panel = jnp.where(inside, (lane == first + sub).astype(f32), rows[k])
        below = coming = upcoming = far = None
        if k + 1 < panels:
            below = [spread(rows[k + 1], first + i) for i in range(BLOCK)]
            coming = [spread(rows[k + 1], after + i) for i in range(BLOCK)]
            upcoming = jnp.where(inside, 0.0, rows[k + 1])
        if near_end > k + 2:
            block = jnp.concatenate(rows[k + 2 : near_end], axis=0)
            far = [spread(block, first + i) for i in range(BLOCK)]
            wide = lax.broadcasted_iota(jnp.int32, block.shape, 1)
            far_rows = jnp.where((wide >= first) & (wide < after), 0.0, block)
        for i in range(BLOCK):
            scale = lax.rsqrt(pivot[i][i : i + 1, :])
            column = pivot[i] * scale
            row = panel[i : i + 1, :] * scale
            entry = [column[j : j + 1, :] for j in range(BLOCK)]
            for j in range(i + 1, BLOCK):
                pivot[j] = pivot[j] - column * entry[j]
            panel = jnp.where(sub == i, row, panel - jnp.where(sub > i, column, 0.0) * row)
            if below is not None:
                lower = below[i] * scale
                for j in range(i + 1, BLOCK):
                    below[j] = below[j] - lower * entry[j]
                for j in range(BLOCK):
                    coming[j] = coming[j] - lower * lower[j : j + 1, :]
                upcoming = upcoming - lower * row
            if far is not None:
                lowest = far[i] * scale
                for j in range(i + 1, BLOCK):
                    far[j] = far[j] - lowest * entry[j]
                far_rows = far_rows - lowest * row
        done.append(jnp.where(lane < after, panel, 0.0))
        pivot = coming
        if below is not None:
            rows[k + 1] = upcoming
        if far is not None:
            for g in range(k + 2, near_end):
                rows[g] = far_rows[BLOCK * (g - k - 2) : BLOCK * (g - k - 1)]
        if near_end < panels:
            high = rounded(panel)
            middle = rounded(panel - high)
            low = rounded(panel - high - middle)
            left = jnp.concatenate([high, high, middle, high, low, middle], axis=0).astype(bf16)
            right = jnp.concatenate([high, middle, high, low, high, middle], axis=0).astype(bf16)
            update = lax.dot_general(
                left, right, (((0,), (0,)), ((), ())), preferred_element_type=f32
            )
            for g in range(near_end, panels):
                rows[g] = jnp.where(inside, 0.0, rows[g]) - update[BLOCK * g : BLOCK * (g + 1)]
    return jnp.concatenate(done, axis=0)


NEAR_PARTS = 4
GROUPS = 3


def kernel(
    leaves, subtrees, slots, samples, probes, near, couplings,
    leaf_out, transfer_out, top_samples, top_probes,
    near_v, probes_v, samples_v, couplings_v, next_probes, handed, handed_in, far1,
    gram, inverse, inner, sent, far_in, corrected, passed, gathered, q_leaf, q_top,
    local_sem, leaf_send, leaf_recv, far_send, far_recv, pass_send, pass_recv,
    join_send, join_recv, last_send, last_recv, out_sem,
):
    levels = leaves.bit_length() - 1
    total = leaves * subtrees
    member = lax.axis_index("leaf")
    cluster = lax.axis_index("clusters")
    mine = cluster * leaves + member

    def along(offset):
        index = lax.rem(mine + offset + total, total)
        return {"leaf": lax.rem(index, leaves), "clusters": index // leaves}

    def across(mask):
        return {"leaf": jnp.bitwise_xor(member, mask), "clusters": cluster}

    def send(source, target, sems, device):
        return pltpu.make_async_remote_copy(
            src_ref=source, dst_ref=target, send_sem=sems[0], recv_sem=sems[1],
            device_id=device, device_id_type=MESH,
        )

    def bit(i):
        return lax.rem(lax.shift_right_logical(member, jnp.int32(i)), 2)

    def share(i):
        return jnp.bitwise_xor(bit(1), bit(3)) if i == 1 and levels > 3 else bit(i)

    def width(t):
        return K >> t

    def begin(t):
        start = jnp.int32(0)
        for i in range(t):
            start = start + share(i) * (K >> (i + 1))
        return pl.multiple_of(start, BLOCK)

    barrier = pltpu.get_barrier_semaphore()
    peers = [along(1), along(-1)]
    for peer in peers:
        pl.semaphore_signal(barrier, inc=1, device_id=peer, device_id_type=MESH)

    fetch_probes = pltpu.make_async_copy(probes, probes_v, local_sem.at[0])
    fetch_samples = pltpu.make_async_copy(samples, samples_v, local_sem.at[1])
    fetch_couplings = pltpu.make_async_copy(couplings, couplings_v, local_sem.at[2])
    fetch_near = []
    for i in range(NEAR_PARTS):
        part = pl.ds(i * (8 * ROWS // NEAR_PARTS), 8 * ROWS // NEAR_PARTS)
        fetch_near.append(pltpu.make_async_copy(near.at[part], near_v.at[part], local_sem.at[3 + i]))
    fetch_probes.start()
    for fetch in fetch_near:
        fetch.start()
    fetch_samples.start()

    def leaf_probes(half):
        return send(
            probes.at[:, K * half : K * (half + 1)], next_probes.at[half],
            (leaf_send.at[half], leaf_recv.at[half]), along(-1),
        )

    def leaf_handed(half):
        return send(
            handed.at[half], handed_in.at[half],
            (leaf_send.at[2 + half], leaf_recv.at[2 + half]), along(1),
        )

    def near_block(which, column):
        return near_v[pl.ds(2 * column + which, ROWS, stride=8), :]

    def times(which, values):
        out = None
        for j in range(0, ROWS // K, 2):
            block = jnp.concatenate([near_block(which, j), near_block(which, j + 1)], axis=1)
            part = product(block, values[K * j : K * (j + 2)])
            out = part if out is None else out + part
        return out

    fetch_probes.wait()
    for fetch in fetch_near:
        fetch.wait()
    fetch_couplings.start()
    pl.semaphore_wait(barrier, len(peers))
    leaf_probes(0).start()
    for j in range(ROWS // K):
        block = product(near_block(1, j), probes_v[...], (0, 0))
        handed[0, K * j : K * (j + 1), :] = block[:, :K]
        handed[1, K * j : K * (j + 1), :] = block[:, K:]
    leaf_handed(0).start()
    leaf_probes(1).start()
    leaf_handed(1).start()
    fetch_samples.wait()
    samples_v[...] = samples_v[...] - times(0, probes_v[...])
    def far_half(half):
        leaf_probes(half).wait_recv()
        upper = jnp.where(mine == total - 1, 0.0, next_probes[half])
        part = samples_v[:, K * half : K * (half + 1)] - times(1, upper)
        leaf_handed(half).wait_recv()
        return part - jnp.where(mine == 0, 0.0, handed_in[half])

    far1[...] = far_half(0)
    block = product(jnp.concatenate([far1[...], probes_v[:, :K]], axis=1), far1[...], (0, 0))
    gram[...] = block[:K]
    inner[2] = block[K:]

    def far_copy(t, group, side):
        n = width(t)
        device = along((2 << t) * (1 - 2 * side))
        if t == 2 and levels > 3:
            device["leaf"] = jnp.bitwise_xor(device["leaf"], 2)
        return send(
            sent.at[t, group, pl.ds(0, n)], far_in.at[side, t, group, pl.ds(0, n)],
            (far_send.at[side, t, group], far_recv.at[side, t, group]), device,
        )

    def pass_copy(t, first, count):
        n = width(t) // 2
        away = pl.multiple_of((1 - share(t)) * n, BLOCK)
        groups = pl.ds(first, count)
        return send(
            sent.at[t, groups, pl.ds(away, n)], passed.at[t, groups, pl.ds(0, n)],
            (pass_send.at[t, first], pass_recv.at[t, first]), across(1 << t),
        )

    def join_copy(t, mask):
        part = corrected.at[t, bit(t), pl.ds(begin(t), width(t))]
        return send(part, part, (join_send.at[t, mask], join_recv.at[t, mask]), across(mask))

    top = levels - 1

    def last_copy(first, count, mask):
        part = gathered.at[pl.ds(first, count), bit(top), pl.ds(begin(top), width(top))]
        return send(part, part, (last_send.at[first, mask], last_recv.at[first, mask]), across(mask))

    def far_order(count):
        return sorted(range(1, count), key=lambda mask: -mask)

    def leaf_second():
        fetch_couplings.wait()
        far2 = far_half(1)
        block = product(jnp.concatenate([far2, probes_v[:, K:]], axis=1), far1[...], (0, 0))
        inner[0] = block[:K]
        inner[1] = block[K:]

    def leaf_basis():
        q_leaf[...] = product(far1[...], inverse[...], (1, 1))
        pltpu.make_async_copy(q_leaf, leaf_out, out_sem.at[levels]).start()

    def level_basis(t):
        x = inverse[...]
        for child in range(2):
            q_top[t, K * child : K * (child + 1), :] = product(corrected[t, child], x, (0, 1))
        pltpu.make_async_copy(q_top.at[t], transfer_out.at[t], out_sem.at[t]).start()

    def kept_pair(t, group):
        h = width(t) // 2
        own = sent[t, group, pl.ds(pl.multiple_of(share(t) * h, BLOCK), h)]
        other = passed[t, group, :h]
        even = bit(t) == 0
        return jnp.concatenate([jnp.where(even, own, other), jnp.where(even, other, own)], axis=1)

    def children(t):
        return jnp.concatenate([corrected[t, 0], corrected[t, 1]], axis=1)

    def coupling_sides(t):
        index = leaves - (leaves >> t) + lax.shift_right_logical(member, jnp.int32(t + 1))
        coupling = couplings_v[slots[index], bit(t)]
        turned = coupling.T
        even = bit(t) == 0
        return jnp.concatenate([jnp.where(even, coupling, turned), jnp.where(even, turned, coupling)], axis=1)

    def correct(t, z, group, sides):
        n = width(t)
        node = lax.shift_right_logical(mine, jnp.int32(t))
        left = jnp.where(node >= 2, far_in[0, t, group, :n], 0.0)
        right = jnp.where(node < (total >> t) - 2, far_in[1, t, group, :n], 0.0)
        return z - product(jnp.concatenate([left, right], axis=1), sides, (1, 1))

    def second_corrected(t, sides):
        far_copy(t, 1, 0).wait_recv()
        far_copy(t, 1, 1).wait_recv()
        n = width(t)
        second = correct(t, sent[t, 0, :n], 1, sides)
        if t == top:
            gathered[0, bit(t), pl.ds(begin(t), n)] = second
            for mask in far_order(leaves):
                last_copy(0, 1, mask).start()
        else:
            sent[t, 0, :n] = second
            pass_copy(t, 0, 1).start()

    def merge(t):
        n = width(t)
        x = inverse[...]
        sent[t, 2, :n] = product(inner[2, :n], x, (1, 1))
        far_copy(t, 2, 0).start()
        far_copy(t, 2, 1).start()
        if t == 0:
            leaf_second()
        else:
            pass_copy(t - 1, 0, 1).wait_recv()
            pairs = jnp.concatenate([kept_pair(t - 1, 0), kept_pair(t - 1, 1)], axis=0)
            block = product(pairs, children(t - 1), (1, 1))
            inner[0, :n] = block[:n]
            inner[1, :n] = block[n:]
        both = product(jnp.concatenate([inner[1, :n], inner[0, :n]], axis=0), x, (1, 1))
        sent[t, 1, :n] = both[:n]
        sent[t, 0, :n] = both[n:]
        far_copy(t, 1, 0).start()
        far_copy(t, 1, 1).start()
        if t == top:
            for group in (1, 2):
                gathered[group, bit(t), pl.ds(begin(t), n)] = sent[t, group, :n]
            for mask in far_order(leaves):
                last_copy(1, 2, mask).start()
        else:
            pass_copy(t, 1, 2).start()
        own = product(gram[pl.ds(begin(t), n)], x, (1, 1))
        sides = coupling_sides(t)
        if t == 0:
            leaf_basis()
        else:
            level_basis(t - 1)

        far_copy(t, 2, 0).wait_recv()
        far_copy(t, 2, 1).wait_recv()
        corrected[t, bit(t), pl.ds(begin(t), n)] = correct(t, own, 2, sides)
        for mask in far_order(2 << t):
            join_copy(t, mask).start()
        if t > 0:
            second_corrected(t, sides)

        for mask in far_order(2 << t):
            join_copy(t, mask).wait_recv()
        wide = children(t)
        if t == top:
            gram[...] = product(wide, wide, (1, 1))
        else:
            pass_copy(t, 1, 2).wait_recv()
            block = product(jnp.concatenate([wide, kept_pair(t, 2)], axis=0), wide, (1, 1))
            gram[...] = block[:K]
            inner[2, : n // 2] = block[K:]

    def last_inner(first, count):
        for mask in far_order(leaves):
            last_copy(first, count, mask).wait_recv()
        wide = jnp.concatenate([corrected[top, 0], corrected[top, 1]], axis=1)
        for group in range(first, first + count):
            pair = jnp.concatenate([gathered[group, 0], gathered[group, 1]], axis=1)
            inner[group] = product(pair, wide, (1, 1))

    def finish():
        x = inverse[...]
        level_basis(levels - 1)
        top_samples[:, :K] = product(x, gram[...], (1, 1))
        last_inner(0, 1)
        block = product(x, jnp.concatenate([inner[group] for group in range(GROUPS)], axis=0), (1, 1))
        top_samples[:, K:] = block[:, :K]
        top_probes[:, K:] = block[:, K : 2 * K]
        top_probes[:, :K] = block[:, 2 * K :]

    def step(s, carry):
        def beside():
            pl.when(s == 1)(lambda: second_corrected(0, coupling_sides(0)))
            pl.when(s == levels)(functools.partial(last_inner, 1, 2))

        inverse[...] = inverse_factor(gram[...], {8: beside})
        for t in range(levels):
            pl.when(s == t)(functools.partial(merge, t))
        pl.when(s == levels)(finish)
        return carry

    lax.fori_loop(0, levels + 1, step, 0)

    for half in range(2):
        leaf_probes(half).wait_send()
        leaf_handed(half).wait_send()
    for t in range(levels):
        for group in (2, 1):
            for side in range(2):
                far_copy(t, group, side).wait_send()
        if t < top:
            pass_copy(t, 0, 1).wait_send()
            pass_copy(t, 1, 2).wait_send()
        for mask in far_order(2 << t):
            join_copy(t, mask).wait_send()
        pltpu.make_async_copy(q_top.at[t], transfer_out.at[t], out_sem.at[t]).wait()
    for mask in far_order(leaves):
        last_copy(1, 2, mask).wait_send()
        last_copy(0, 1, mask).wait_send()
    pltpu.make_async_copy(q_leaf, leaf_out, out_sem.at[levels]).wait()


def hand_out(*refs):
    count = len(refs) // 2
    for i in range(count):
        refs[count + i][...] = refs[i][...]


def solution(mesh):
    leaves, subtrees = mesh.shape["leaf"], mesh.shape["clusters"]
    levels = leaves.bit_length() - 1

    def body(samples, probes, near_blocks, couplings, node_slot):
        near = near_blocks.reshape(ROWS, 2, ROWS // K, K).transpose(0, 2, 1, 3).reshape(-1, K)
        anywhere = pl.BlockSpec(memory_space=pl.ANY)
        vmem = pl.BlockSpec(memory_space=pltpu.VMEM)
        shapes = (
            jax.ShapeDtypeStruct((ROWS, K), f32),
            jax.ShapeDtypeStruct((levels, 2 * K, K), f32),
            jax.ShapeDtypeStruct((K, 2 * K), f32),
            jax.ShapeDtypeStruct((K, 2 * K), f32),
        )
        dma = pltpu.SemaphoreType.DMA
        results = pl.pallas_call(
            functools.partial(kernel, leaves, subtrees),
            out_shape=shapes,
            in_specs=[pl.BlockSpec(memory_space=pltpu.SMEM)] + [anywhere] * 4,
            out_specs=(anywhere, anywhere, vmem, vmem),
            scratch_shapes=[
                pltpu.VMEM((8 * ROWS, K), f32),
                pltpu.VMEM((ROWS, 2 * K), f32),
                pltpu.VMEM((ROWS, 2 * K), f32),
                pltpu.VMEM(couplings.shape[1:], f32),
                pltpu.VMEM((2, ROWS, K), f32),
                pltpu.VMEM((2, ROWS, K), f32),
                pltpu.VMEM((2, ROWS, K), f32),
                pltpu.VMEM((ROWS, K), f32),
                pltpu.VMEM((K, K), f32),
                pltpu.VMEM((K, K), f32),
                pltpu.VMEM((GROUPS, K, K), f32),
                pltpu.VMEM((levels, GROUPS, K, K), f32),
                pltpu.VMEM((2, levels, GROUPS, K, K), f32),
                pltpu.VMEM((levels, 2, K, K), f32),
                pltpu.VMEM((levels, GROUPS, K // 2, K), f32),
                pltpu.VMEM((GROUPS, 2, K, K), f32),
                pltpu.VMEM((ROWS, K), f32),
                pltpu.VMEM((levels, 2 * K, K), f32),
                dma((3 + NEAR_PARTS,)), dma((4,)), dma((4,)),
                dma((2, levels, GROUPS)), dma((2, levels, GROUPS)),
                dma((levels, 2)), dma((levels, 2)),
                dma((levels, leaves)), dma((levels, leaves)),
                dma((2, leaves)), dma((2, leaves)),
                dma((levels + 1,)),
            ],
            compiler_params=pltpu.CompilerParams(
                collective_id=0, has_side_effects=True, vmem_limit_bytes=60 * 2**20
            ),
            name="nested_bases",
        )(node_slot[0], samples, probes, near, couplings[0])
        leaf_basis, transfer, top_samples, top_probes = pl.pallas_call(
            hand_out,
            out_shape=shapes,
            in_specs=[vmem] * 4,
            out_specs=(vmem,) * 4,
            name="hand_out",
        )(*results)
        return leaf_basis, transfer[None], top_samples[None], top_probes[None]

    in_specs = (
        P(("clusters", "leaf"), None),
        P(("clusters", "leaf"), None),
        P(("clusters", "leaf"), None, None),
        P("clusters", None, None, None, None),
        P("clusters", None),
    )
    out_specs = (
        P(("clusters", "leaf"), None),
        P(("clusters", "leaf"), None, None, None),
        P("clusters", None, None),
        P("clusters", None, None),
    )
    return jax.shard_map(body, mesh=mesh, in_specs=in_specs, out_specs=out_specs, check_vma=False)
```

```python
import functools

import jax
import jax.numpy as jnp
from jax import lax
from jax.experimental import pallas as pl
from jax.experimental.pallas import tpu as pltpu
from jax.sharding import PartitionSpec as P

MESH = pl.DeviceIdType.MESH
f32 = jnp.float32
bf16 = jnp.bfloat16

K = 128
ROWS = 512
BLOCK = 8
REACH = 3


def halves(value):
    high = value.astype(bf16)
    return high, (value - high.astype(f32)).astype(bf16)


def product(a, b, contract=(1, 0)):
    dims = (((contract[0],), (contract[1],)), ((), ()))
    a_high, a_low = halves(a)
    b_high, b_low = halves(b)
    dot = functools.partial(lax.dot_general, dimension_numbers=dims, preferred_element_type=f32)
    return dot(a_high, b_high) + (dot(a_high, b_low) + dot(a_low, b_high))


def spread(block, column):
    return jnp.broadcast_to(block[:, column : column + 1], (block.shape[0], K))


def inverse_factor(gram):
    panels = K // BLOCK
    lane = lax.broadcasted_iota(jnp.int32, (BLOCK, K), 1)
    sub = lax.broadcasted_iota(jnp.int32, (BLOCK, K), 0)
    rounded = lambda v: v.astype(bf16).astype(f32)
    rows = [gram[BLOCK * g : BLOCK * (g + 1)] for g in range(panels)]
    pivot = [spread(rows[0], i) for i in range(BLOCK)]
    done = []
    for k in range(panels):
        first, after = BLOCK * k, BLOCK * (k + 1)
        near_end = min(panels, k + 1 + REACH)
        inside = (lane >= first) & (lane < after)
        panel = jnp.where(inside, (lane == first + sub).astype(f32), rows[k])
        below = coming = upcoming = far = None
        if k + 1 < panels:
            below = [spread(rows[k + 1], first + i) for i in range(BLOCK)]
            coming = [spread(rows[k + 1], after + i) for i in range(BLOCK)]
            upcoming = jnp.where(inside, 0.0, rows[k + 1])
        if near_end > k + 2:
            block = jnp.concatenate(rows[k + 2 : near_end], axis=0)
            far = [spread(block, first + i) for i in range(BLOCK)]
            wide = lax.broadcasted_iota(jnp.int32, block.shape, 1)
            far_rows = jnp.where((wide >= first) & (wide < after), 0.0, block)
        for i in range(BLOCK):
            scale = lax.rsqrt(pivot[i][i : i + 1, :])
            column = pivot[i] * scale
            row = panel[i : i + 1, :] * scale
            entry = [column[j : j + 1, :] for j in range(BLOCK)]
            for j in range(i + 1, BLOCK):
                pivot[j] = pivot[j] - column * entry[j]
            panel = jnp.where(sub == i, row, panel - jnp.where(sub > i, column, 0.0) * row)
            if below is not None:
                lower = below[i] * scale
                for j in range(i + 1, BLOCK):
                    below[j] = below[j] - lower * entry[j]
                for j in range(BLOCK):
                    coming[j] = coming[j] - lower * lower[j : j + 1, :]
                upcoming = upcoming - lower * row
            if far is not None:
                lowest = far[i] * scale
                for j in range(i + 1, BLOCK):
                    far[j] = far[j] - lowest * entry[j]
                far_rows = far_rows - lowest * row
        done.append(jnp.where(lane < after, panel, 0.0))
        pivot = coming
        if below is not None:
            rows[k + 1] = upcoming
        if far is not None:
            for g in range(k + 2, near_end):
                rows[g] = far_rows[BLOCK * (g - k - 2) : BLOCK * (g - k - 1)]
        if near_end < panels:
            high = rounded(panel)
            middle = rounded(panel - high)
            low = rounded(panel - high - middle)
            left = jnp.concatenate([high, high, middle, high, low, middle], axis=0).astype(bf16)
            right = jnp.concatenate([high, middle, high, low, high, middle], axis=0).astype(bf16)
            update = lax.dot_general(
                left, right, (((0,), (0,)), ((), ())), preferred_element_type=f32
            )
            for g in range(near_end, panels):
                rows[g] = jnp.where(inside, 0.0, rows[g]) - update[BLOCK * g : BLOCK * (g + 1)]
    return jnp.concatenate(done, axis=0)


NEAR_PARTS = 4
GROUPS = 3


def kernel(
    leaves, subtrees, slots, samples, probes, near, couplings,
    leaf_out, transfer_out, top_samples, top_probes,
    near_v, probes_v, samples_v, couplings_v, next_probes, handed, handed_in, far1,
    gram, inverse, inner, sent, far_in, corrected, passed, gathered, q_leaf, q_top,
    local_sem, leaf_send, leaf_recv, far_send, far_recv, pass_send, pass_recv,
    join_send, join_recv, last_send, last_recv, out_sem,
):
    levels = leaves.bit_length() - 1
    total = leaves * subtrees
    member = lax.axis_index("leaf")
    cluster = lax.axis_index("clusters")
    mine = cluster * leaves + member

    def along(offset):
        index = lax.rem(mine + offset + total, total)
        return {"leaf": lax.rem(index, leaves), "clusters": index // leaves}

    def across(mask):
        return {"leaf": jnp.bitwise_xor(member, mask), "clusters": cluster}

    def send(source, target, sems, device):
        return pltpu.make_async_remote_copy(
            src_ref=source, dst_ref=target, send_sem=sems[0], recv_sem=sems[1],
            device_id=device, device_id_type=MESH,
        )

    def bit(i):
        return lax.rem(lax.shift_right_logical(member, jnp.int32(i)), 2)

    def share(i):
        return jnp.bitwise_xor(bit(1), bit(3)) if i == 1 and levels > 3 else bit(i)

    def width(t):
        return K >> t

    def begin(t):
        start = jnp.int32(0)
        for i in range(t):
            start = start + share(i) * (K >> (i + 1))
        return pl.multiple_of(start, BLOCK)

    barrier = pltpu.get_barrier_semaphore()
    peers = [along(1), along(-1)]
    for peer in peers:
        pl.semaphore_signal(barrier, inc=1, device_id=peer, device_id_type=MESH)

    fetch_probes = pltpu.make_async_copy(probes, probes_v, local_sem.at[0])
    fetch_samples = pltpu.make_async_copy(samples, samples_v, local_sem.at[1])
    fetch_couplings = pltpu.make_async_copy(couplings, couplings_v, local_sem.at[2])
    fetch_near = []
    for i in range(NEAR_PARTS):
        part = pl.ds(i * (8 * ROWS // NEAR_PARTS), 8 * ROWS // NEAR_PARTS)
        fetch_near.append(pltpu.make_async_copy(near.at[part], near_v.at[part], local_sem.at[3 + i]))
    fetch_probes.start()
    for fetch in fetch_near:
        fetch.start()
    fetch_samples.start()

    def leaf_probes(half):
        return send(
            probes.at[:, K * half : K * (half + 1)], next_probes.at[half],
            (leaf_send.at[half], leaf_recv.at[half]), along(-1),
        )

    def leaf_handed(half):
        return send(
            handed.at[half], handed_in.at[half],
            (leaf_send.at[2 + half], leaf_recv.at[2 + half]), along(1),
        )

    def near_block(which, column):
        return near_v[pl.ds(2 * column + which, ROWS, stride=8), :]

    def times(which, values):
        out = None
        for j in range(0, ROWS // K, 2):
            block = jnp.concatenate([near_block(which, j), near_block(which, j + 1)], axis=1)
            part = product(block, values[K * j : K * (j + 2)])
            out = part if out is None else out + part
        return out

    fetch_probes.wait()
    for fetch in fetch_near:
        fetch.wait()
    fetch_couplings.start()
    pl.semaphore_wait(barrier, len(peers))
    leaf_probes(0).start()
    for j in range(ROWS // K):
        block = product(near_block(1, j), probes_v[...], (0, 0))
        handed[0, K * j : K * (j + 1), :] = block[:, :K]
        handed[1, K * j : K * (j + 1), :] = block[:, K:]
    leaf_handed(0).start()
    leaf_probes(1).start()
    leaf_handed(1).start()
    fetch_samples.wait()
    samples_v[...] = samples_v[...] - times(0, probes_v[...])
    def far_half(half):
        leaf_probes(half).wait_recv()
        upper = jnp.where(mine == total - 1, 0.0, next_probes[half])
        part = samples_v[:, K * half : K * (half + 1)] - times(1, upper)
        leaf_handed(half).wait_recv()
        return part - jnp.where(mine == 0, 0.0, handed_in[half])

    far1[...] = far_half(0)
    block = product(jnp.concatenate([far1[...], probes_v[:, :K]], axis=1), far1[...], (0, 0))
    gram[...] = block[:K]
    inner[2] = block[K:]

    def far_copy(t, group, side):
        n = width(t)
        device = along((2 << t) * (1 - 2 * side))
        if t == 2 and levels > 3:
            device["leaf"] = jnp.bitwise_xor(device["leaf"], 2)
        return send(
            sent.at[t, group, pl.ds(0, n)], far_in.at[side, t, group, pl.ds(0, n)],
            (far_send.at[side, t, group], far_recv.at[side, t, group]), device,
        )

    def pass_copy(t, first, count):
        n = width(t) // 2
        away = pl.multiple_of((1 - share(t)) * n, BLOCK)
        groups = pl.ds(first, count)
        return send(
            sent.at[t, groups, pl.ds(away, n)], passed.at[t, groups, pl.ds(0, n)],
            (pass_send.at[t, first], pass_recv.at[t, first]), across(1 << t),
        )

    def join_copy(t, mask):
        part = corrected.at[t, bit(t), pl.ds(begin(t), width(t))]
        return send(part, part, (join_send.at[t, mask], join_recv.at[t, mask]), across(mask))

    top = levels - 1

    def last_copy(first, count, mask):
        part = gathered.at[pl.ds(first, count), bit(top), pl.ds(begin(top), width(top))]
        return send(part, part, (last_send.at[first, mask], last_recv.at[first, mask]), across(mask))

    def far_order(count):
        return sorted(range(1, count), key=lambda mask: -mask)

    def leaf_second():
        far2 = far_half(1)
        block = product(jnp.concatenate([far2, probes_v[:, K:]], axis=1), far1[...], (0, 0))
        inner[0] = block[:K]
        inner[1] = block[K:]

    def leaf_basis():
        q_leaf[...] = product(far1[...], inverse[...], (1, 1))
        pltpu.make_async_copy(q_leaf, leaf_out, out_sem.at[levels]).start()

    def level_basis(t):
        x = inverse[...]
        for child in range(2):
            q_top[t, K * child : K * (child + 1), :] = product(corrected[t, child], x, (0, 1))
        pltpu.make_async_copy(q_top.at[t], transfer_out.at[t], out_sem.at[t]).start()

    def kept_pair(t, group):
        h = width(t) // 2
        own = sent[t, group, pl.ds(pl.multiple_of(share(t) * h, BLOCK), h)]
        other = passed[t, group, :h]
        even = bit(t) == 0
        return jnp.concatenate([jnp.where(even, own, other), jnp.where(even, other, own)], axis=1)

    def children(t):
        return jnp.concatenate([corrected[t, 0], corrected[t, 1]], axis=1)

    def coupling_sides(t):
        index = leaves - (leaves >> t) + lax.shift_right_logical(member, jnp.int32(t + 1))
        coupling = couplings_v[slots[index], bit(t)]
        turned = coupling.T
        even = bit(t) == 0
        return jnp.concatenate([jnp.where(even, coupling, turned), jnp.where(even, turned, coupling)], axis=1)

    def correct(t, z, group, sides):
        n = width(t)
        node = lax.shift_right_logical(mine, jnp.int32(t))
        left = jnp.where(node >= 2, far_in[0, t, group, :n], 0.0)
        right = jnp.where(node < (total >> t) - 2, far_in[1, t, group, :n], 0.0)
        return z - product(jnp.concatenate([left, right], axis=1), sides, (1, 1))

    def second_corrected(t, sides):
        far_copy(t, 1, 0).wait_recv()
        far_copy(t, 1, 1).wait_recv()
        n = width(t)
        second = correct(t, sent[t, 0, :n], 1, sides)
        if t == top:
            gathered[0, bit(t), pl.ds(begin(t), n)] = second
            for mask in far_order(leaves):
                last_copy(0, 1, mask).start()
        else:
            sent[t, 0, :n] = second
            pass_copy(t, 0, 1).start()

    def merge(t):
        n = width(t)
        x = inverse[...]
        sent[t, 2, :n] = product(inner[2, :n], x, (1, 1))
        far_copy(t, 2, 0).start()
        far_copy(t, 2, 1).start()
        if t == 0:
            fetch_couplings.wait()
        if t == 1:
            second_corrected(0, coupling_sides(0))
        own = product(gram[pl.ds(begin(t), n)], x, (1, 1))
        sides = coupling_sides(t)
        if t == 0:
            leaf_second()
        else:
            if t == 1:
                level_basis(0)
            pass_copy(t - 1, 0, 1).wait_recv()
            pairs = jnp.concatenate([kept_pair(t - 1, 0), kept_pair(t - 1, 1)], axis=0)
            block = product(pairs, children(t - 1), (1, 1))
            inner[0, :n] = block[:n]
            inner[1, :n] = block[n:]
        both = product(jnp.concatenate([inner[1, :n], inner[0, :n]], axis=0), x, (1, 1))
        sent[t, 1, :n] = both[:n]
        sent[t, 0, :n] = both[n:]
        far_copy(t, 1, 0).start()
        far_copy(t, 1, 1).start()
        if t == top:
            for group in (1, 2):
                gathered[group, bit(t), pl.ds(begin(t), n)] = sent[t, group, :n]
            for mask in far_order(leaves):
                last_copy(1, 2, mask).start()
        else:
            pass_copy(t, 1, 2).start()
        if t == 0:
            leaf_basis()
        elif t > 1:
            level_basis(t - 1)

        far_copy(t, 2, 0).wait_recv()
        far_copy(t, 2, 1).wait_recv()
        corrected[t, bit(t), pl.ds(begin(t), n)] = correct(t, own, 2, sides)
        for mask in far_order(2 << t):
            join_copy(t, mask).start()
        if t > 0:
            second_corrected(t, sides)

        for mask in far_order(2 << t):
            join_copy(t, mask).wait_recv()
        wide = children(t)
        if t == top:
            gram[...] = product(wide, wide, (1, 1))
        else:
            pass_copy(t, 1, 2).wait_recv()
            block = product(jnp.concatenate([wide, kept_pair(t, 2)], axis=0), wide, (1, 1))
            gram[...] = block[:K]
            inner[2, : n // 2] = block[K:]

    def last_inner(first, count):
        for mask in far_order(leaves):
            last_copy(first, count, mask).wait_recv()
        wide = jnp.concatenate([corrected[top, 0], corrected[top, 1]], axis=1)
        for group in range(first, first + count):
            pair = jnp.concatenate([gathered[group, 0], gathered[group, 1]], axis=1)
            inner[group] = product(pair, wide, (1, 1))

    def finish():
        x = inverse[...]
        level_basis(levels - 1)
        top_samples[:, :K] = product(x, gram[...], (1, 1))
        last_inner(1, 2)
        last_inner(0, 1)
        block = product(x, jnp.concatenate([inner[group] for group in range(GROUPS)], axis=0), (1, 1))
        top_samples[:, K:] = block[:, :K]
        top_probes[:, K:] = block[:, K : 2 * K]
        top_probes[:, :K] = block[:, 2 * K :]

    def step(s, carry):
        inverse[...] = inverse_factor(gram[...])
        for t in range(levels):
            pl.when(s == t)(functools.partial(merge, t))
        pl.when(s == levels)(finish)
        return carry

    lax.fori_loop(0, levels + 1, step, 0)

    for half in range(2):
        leaf_probes(half).wait_send()
        leaf_handed(half).wait_send()
    for t in range(levels):
        for group in (2, 1):
            for side in range(2):
                far_copy(t, group, side).wait_send()
        if t < top:
            pass_copy(t, 0, 1).wait_send()
            pass_copy(t, 1, 2).wait_send()
        for mask in far_order(2 << t):
            join_copy(t, mask).wait_send()
        pltpu.make_async_copy(q_top.at[t], transfer_out.at[t], out_sem.at[t]).wait()
    for mask in far_order(leaves):
        last_copy(1, 2, mask).wait_send()
        last_copy(0, 1, mask).wait_send()
    pltpu.make_async_copy(q_leaf, leaf_out, out_sem.at[levels]).wait()


def hand_out(levels, *refs):
    sources, targets, held, (in_sem, out_sem) = refs[:4], refs[4:8], refs[8:12], refs[12:]
    pieces = [(1, t) for t in range(levels)] + [(0, None), (2, None), (3, None)]
    pick = lambda ref, t: ref if t is None else ref.at[t]
    reads = [
        pltpu.make_async_copy(pick(sources[i], t), pick(held[i], t), in_sem.at[n])
        for n, (i, t) in enumerate(pieces)
    ]
    writes = [
        pltpu.make_async_copy(pick(held[i], t), pick(targets[i], t), out_sem.at[n])
        for n, (i, t) in enumerate(pieces)
    ]
    for read in reads:
        read.start()
    for read, write in zip(reads, writes):
        read.wait()
        write.start()
    for write in writes:
        write.wait()


def solution(mesh):
    leaves, subtrees = mesh.shape["leaf"], mesh.shape["clusters"]
    levels = leaves.bit_length() - 1

    def body(samples, probes, near_blocks, couplings, node_slot):
        near = near_blocks.reshape(ROWS, 2, ROWS // K, K).transpose(0, 2, 1, 3).reshape(-1, K)
        anywhere = pl.BlockSpec(memory_space=pl.ANY)
        vmem = pl.BlockSpec(memory_space=pltpu.VMEM)
        shapes = (
            jax.ShapeDtypeStruct((ROWS, K), f32),
            jax.ShapeDtypeStruct((levels, 2 * K, K), f32),
            jax.ShapeDtypeStruct((K, 2 * K), f32),
            jax.ShapeDtypeStruct((K, 2 * K), f32),
        )
        dma = pltpu.SemaphoreType.DMA
        results = pl.pallas_call(
            functools.partial(kernel, leaves, subtrees),
            out_shape=shapes,
            in_specs=[pl.BlockSpec(memory_space=pltpu.SMEM)] + [anywhere] * 4,
            out_specs=(anywhere, anywhere, vmem, vmem),
            scratch_shapes=[
                pltpu.VMEM((8 * ROWS, K), f32),
                pltpu.VMEM((ROWS, 2 * K), f32),
                pltpu.VMEM((ROWS, 2 * K), f32),
                pltpu.VMEM(couplings.shape[1:], f32),
                pltpu.VMEM((2, ROWS, K), f32),
                pltpu.VMEM((2, ROWS, K), f32),
                pltpu.VMEM((2, ROWS, K), f32),
                pltpu.VMEM((ROWS, K), f32),
                pltpu.VMEM((K, K), f32),
                pltpu.VMEM((K, K), f32),
                pltpu.VMEM((GROUPS, K, K), f32),
                pltpu.VMEM((levels, GROUPS, K, K), f32),
                pltpu.VMEM((2, levels, GROUPS, K, K), f32),
                pltpu.VMEM((levels, 2, K, K), f32),
                pltpu.VMEM((levels, GROUPS, K // 2, K), f32),
                pltpu.VMEM((GROUPS, 2, K, K), f32),
                pltpu.VMEM((ROWS, K), f32),
                pltpu.VMEM((levels, 2 * K, K), f32),
                dma((3 + NEAR_PARTS,)), dma((4,)), dma((4,)),
                dma((2, levels, GROUPS)), dma((2, levels, GROUPS)),
                dma((levels, 2)), dma((levels, 2)),
                dma((levels, leaves)), dma((levels, leaves)),
                dma((2, leaves)), dma((2, leaves)),
                dma((levels + 1,)),
            ],
            compiler_params=pltpu.CompilerParams(
                collective_id=0, has_side_effects=True, vmem_limit_bytes=60 * 2**20
            ),
            name="nested_bases",
        )(node_slot[0], samples, probes, near, couplings[0])
        leaf_basis, transfer, top_samples, top_probes = pl.pallas_call(
            functools.partial(hand_out, levels),
            out_shape=shapes,
            in_specs=[anywhere] * 4,
            out_specs=(anywhere,) * 4,
            scratch_shapes=[pltpu.VMEM(shape.shape, f32) for shape in shapes] + [dma((levels + 3,))] * 2,
            name="hand_out",
        )(*results)
        return leaf_basis, transfer[None], top_samples[None], top_probes[None]

    in_specs = (
        P(("clusters", "leaf"), None),
        P(("clusters", "leaf"), None),
        P(("clusters", "leaf"), None, None),
        P("clusters", None, None, None, None),
        P("clusters", None),
    )
    out_specs = (
        P(("clusters", "leaf"), None),
        P(("clusters", "leaf"), None, None, None),
        P("clusters", None, None),
        P("clusters", None, None),
    )
    return jax.shard_map(body, mesh=mesh, in_specs=in_specs, out_specs=out_specs, check_vma=False)
```
